256 devices in a mesh: row: 32 (over z_lo, y, core), col: 8 (over z_hi, x).
Axes of the slice: x: 4, y: 4, z: 8 (z_hi: 2, z_lo: 4; z = z_hi * 4 + z_lo), core: 2. Of those that a mesh axis runs over, the one named last changes fastest.
Arguments:
- damping: bfloat16 [1536, 128, 1536], P('col', 'row'), may hold values from -60 to 60
- block_seeds: int32 [32], replicated, may hold values from 1 to 65520
Outputs:
- basis: float32 [32, 1536, 32], P('row', 'col')
The draws below stay inside these ranges and needn't reach their ends.
All inputs are finite; a program needn't handle non-finite values.
Results may differ from the reference program's by a relative error of at most 0.0057.
Values may be sent and summed in bfloat16 or wider, within the bound.
A program may use at most 64 MiB of HBM per device.

```python
import math
import jax
import jax.numpy as jnp
from jax import lax

NF = 128
M = 1536
P_SIZE = 32
NB = 32
NSTEPS = 12


def draw_damping(key, part):
    col_idx = jnp.arange(M, dtype=jnp.float32)[:, None, None]
    col_scale = jnp.exp(jnp.log(3.0) * col_idx / M)
    values = jnp.clip(jax.random.normal(key, (M, NF, M), jnp.float32), -5.0, 5.0)
    return (values * col_scale).astype(jnp.bfloat16)


def with_ends(entries, own_key, least, largest):
    index_at = [jax.random.randint(jax.random.fold_in(own_key, axis), (), 0, length) for axis, length in enumerate(entries.shape)]
    longest = entries.shape.index(max(entries.shape))
    neighbour = index_at[:longest] + [(index_at[longest] + 1) % entries.shape[longest]] + index_at[longest + 1:]
    return entries.at[tuple(index_at)].set(least).at[tuple(neighbour)].set(largest)


def setup_inputs(seed: int = 0) -> dict:
    arg_keys = jax.random.split(jax.random.key(seed), 3)
    return {
        "damping": draw_damping(jax.random.fold_in(arg_keys[2], 71), 0),
        "block_seeds": with_ends(jax.random.randint(arg_keys[1], (NB,), 1, 65521), jax.random.fold_in(arg_keys[1], 1), 1, 65520).astype(jnp.int32),
    }


def lag_table():
    lag_idx = jnp.arange(2 * NB, dtype=jnp.float32)[:, None]
    freq_idx = jnp.arange(NF, dtype=jnp.float32)[None, :]
    window = jnp.exp(-math.log(3.0) * lag_idx / NB)
    cos_table = jnp.cos(math.pi * (freq_idx + 0.5) * lag_idx / NF) * window * math.sqrt(2.0 / NF) / math.sqrt(NB * M)
    return cos_table.astype(jnp.bfloat16)

def probe_blocks(block_seeds, start_col, number):
    prime_mod = 65521
    column = (start_col + jnp.arange(number, dtype=jnp.int32))[None, :, None]
    probe_col = jnp.arange(P_SIZE, dtype=jnp.int32)[None, None, :]
    seed_col = block_seeds.astype(jnp.int32)[:, None, None]
    inner_part = seed_col * (column + 1) % prime_mod * (column + 3) % prime_mod
    phase_val = (inner_part * (probe_col + 1) + seed_col * (probe_col + 1) % prime_mod * (probe_col + 2)) % prime_mod
    return jnp.cos(2.0 * math.pi * phase_val.astype(jnp.float32) / prime_mod).astype(jnp.bfloat16)

def hankel_stack(blocks, group_len):
    extent = blocks.shape[0] + group_len - 1
    padded = jnp.pad(blocks, ((group_len - 1, group_len - 1), (0, 0), (0, 0)))
    shifted = [padded[group_len - 1 - offset:group_len - 1 - offset + extent] for offset in range(group_len)]
    return jnp.stack(shifted, axis=2).reshape(extent, blocks.shape[1], group_len * blocks.shape[2])

def hankel_pass(lags_all, stack, shift_by, form, group_len):
    extent = stack.shape[0]
    stack_wide = stack.astype(jnp.float32)
    pieces = []
    for group in range(NB // group_len):
        start_lag = group * group_len + shift_by
        window_lags = lags_all[start_lag:start_lag + extent].astype(jnp.float32)
        product = jnp.einsum(form, window_lags, stack_wide)
        pieces.append(product.reshape(product.shape[0], group_len, P_SIZE).transpose(1, 0, 2))
    return jnp.concatenate(pieces, axis=0)

def finish(mine, gram):
    highest = lax.Precision.HIGHEST
    scale = jnp.trace(gram) + 1e-06
    current = gram / scale
    eye_mat = jnp.eye(P_SIZE, dtype=jnp.float32)
    inverse = eye_mat
    for repeat in range(NSTEPS):
        weight = 1.5 * eye_mat - 0.5 * jnp.dot(inverse, current, precision=highest)
        current = jnp.dot(current, weight, precision=highest)
        inverse = jnp.dot(weight, inverse, precision=highest)
    factor = math.sqrt(NB * M) / jnp.sqrt(scale)
    return factor * jnp.einsum('bcp,pq->bcq', mine, inverse, precision=highest)

def reference(damping, block_seeds):
    group_len = min(16, NB)
    cos_table = lag_table()
    by_freq = jnp.transpose(damping, (1, 2, 0)).reshape(NF, M * M)
    lags_all = jnp.dot(cos_table, by_freq, preferred_element_type=jnp.float32)
    lags_all = lags_all.astype(jnp.bfloat16).reshape(2 * NB, M, M)
    probes = probe_blocks(block_seeds, 0, M)
    forward = hankel_pass(lags_all, hankel_stack(probes, group_len), 0, 'lrc,lcn->rn', group_len)
    forward_b = forward.astype(jnp.bfloat16)
    backward = hankel_pass(lags_all, hankel_stack(forward_b, group_len), 1, 'lrc,lrn->cn', group_len)
    gram = jnp.einsum('bcp,bcq->pq', backward, backward, precision=lax.Precision.HIGHEST)
    return finish(backward, gram)
```

```python
import math

import jax
import jax.numpy as jnp
from jax import lax
from jax.sharding import PartitionSpec as P

NF = 128
M = 1536
P_SIZE = 32
NB = 32
NSTEPS = 12
PRIME = 65521


def probe_blocks(block_seeds, start_col, number):
    column = (start_col + jnp.arange(number, dtype=jnp.int32))[None, None, :]
    probe_col = jnp.arange(P_SIZE, dtype=jnp.int32)[None, :, None]
    seed = block_seeds[:, None, None]
    inner = seed * (column + 1) % PRIME * (column + 3) % PRIME
    second = seed * (probe_col + 1) % PRIME * (probe_col + 2)
    phase = (inner * (probe_col + 1) + second).astype(jnp.float32)
    phase = phase - jnp.round(phase * (1.0 / PRIME)) * PRIME
    return jnp.cos((2.0 * math.pi / PRIME) * phase).astype(jnp.bfloat16)


def wave(freq, step, sign):
    angle = (math.pi / NF) * (freq[:, None] + 0.5) * step[None, :]
    window = jnp.exp(-math.log(3.0) * step / NB)[None, :]
    both = jnp.stack([jnp.cos(angle) * window, sign * jnp.sin(angle) * window], 1)
    return both.reshape(2 * freq.shape[0], step.shape[0])


def finish(mine, gram):
    highest = lax.Precision.HIGHEST
    scale = jnp.trace(gram) + 1e-06
    current = gram / scale
    eye_mat = jnp.eye(P_SIZE, dtype=jnp.float32)
    inverse = eye_mat
    for repeat in range(NSTEPS):
        weight = 1.5 * eye_mat - 0.5 * jnp.dot(inverse, current, precision=highest)
        current = jnp.dot(current, weight, precision=highest)
        inverse = jnp.dot(weight, inverse, precision=highest)
    factor = math.sqrt(NB * M) / jnp.sqrt(scale)
    return factor * jnp.einsum("pc,pq->cq", mine, inverse, precision=highest)


def shards(damping, block_seeds):
    highest = lax.Precision.HIGHEST
    rows, cols = lax.axis_size("row"), lax.axis_size("col")
    tile, own = damping.shape[0], damping.shape[1]
    strip = M // cols // rows
    steps = jnp.arange(NB, dtype=jnp.float32)
    every = jnp.arange(NF, dtype=jnp.float32)
    mine = (lax.axis_index("row") * own + jnp.arange(own)).astype(jnp.float32)
    amp = math.sqrt(2.0 / NF) / math.sqrt(NB * M)

    probes = probe_blocks(block_seeds, lax.axis_index("col") * tile, tile)
    table = wave(mine, steps, 1.0).astype(jnp.bfloat16)
    mixed = jnp.einsum("kj,jpc->kpc", table, probes, preferred_element_type=jnp.float32)
    mixed = mixed.astype(jnp.bfloat16).reshape(own, 2, P_SIZE, tile)
    part = jnp.einsum("kspc,ckr->rksp", mixed, damping, preferred_element_type=jnp.float32)
    part = part.astype(jnp.bfloat16).reshape(M, 2 * own * P_SIZE)
    part = lax.psum_scatter(part, "col", scatter_dimension=0, tiled=True)
    part = lax.all_to_all(part.reshape(rows, strip, 2 * own, P_SIZE), "row", 0, 0, tiled=True)
    forward = jnp.einsum(
        "aki,ajkp->ijp",
        (amp * wave(every, steps, -1.0)).reshape(rows, 2 * own, NB),
        part.astype(jnp.float32),
        precision=highest,
    )
    forward_b = forward.astype(jnp.bfloat16)
    spread = jnp.einsum(
        "aki,ijp->ajkp",
        (amp * wave(every, steps + 1.0, 1.0)).reshape(rows, 2 * own, NB),
        forward_b.astype(jnp.float32),
        precision=highest,
    ).astype(jnp.bfloat16)
    spread = lax.all_to_all(spread, "row", 0, 0, tiled=True)
    spread = lax.all_gather(spread.reshape(M // cols, 2 * own * P_SIZE), "col", axis=0, tiled=True)
    back = jnp.einsum(
        "ckr,rksp->cksp",
        damping,
        spread.reshape(M, own, 2, P_SIZE),
        preferred_element_type=jnp.float32,
    ).astype(jnp.bfloat16)
    back = lax.all_to_all(back.reshape(rows, strip, 2 * own, P_SIZE), "row", 0, 0, tiled=True)
    backward = jnp.einsum(
        "akj,ackp->jpc",
        wave(every, steps, -1.0).reshape(rows, 2 * own, NB),
        back.astype(jnp.float32),
        precision=highest,
    )
    gram = jnp.einsum("jpc,jqc->pq", backward, backward, precision=highest)
    gram = lax.psum(gram, ("row", "col"))
    block = lax.all_to_all(backward, "row", 0, 2, tiled=True)
    return finish(block[0], gram)[None]


def solution(mesh):
    return jax.shard_map(
        shards,
        mesh=mesh,
        in_specs=(P("col", "row", None), P()),
        out_specs=P("row", "col", None),
        check_vma=False,
    )
```

```python
import functools
import math

import jax
import jax.numpy as jnp
import numpy as np
from jax import lax
from jax.experimental import pallas as pl
from jax.experimental.pallas import tpu as pltpu
from jax.sharding import PartitionSpec as P

NF = 128
M = 1536
PS = 32
NB = 32
NSTEPS = 12
PRIME = 65521
OWN = 4
KC = 2 * OWN
ROWS = 32
TILE = 192
NX, NY, NZ = 4, 4, 8
CHUNKS = 3
MESH = pl.DeviceIdType.MESH
F32, BF16 = jnp.float32, jnp.bfloat16
HIGHEST = lax.Precision.HIGHEST


def wave(step, sign):
    freq = np.arange(NF)[:, None] + 0.5
    angle = math.pi * freq * step[None, :] / NF
    window = np.exp(-math.log(3.0) * step / NB)[None, :]
    return np.stack([np.cos(angle) * window, sign * np.sin(angle) * window], 1).reshape(2 * NF, len(step))


def halves(table):
    high = table.astype(jnp.bfloat16)
    low = (table - high.astype(np.float64)).astype(jnp.bfloat16)
    return high, low


def tables():
    step = np.arange(NB).astype(np.float64)
    amp = math.sqrt(2.0 / NF) / math.sqrt(NB * M)
    mix = np.repeat(wave(step, 1.0), PS, axis=1).astype(np.float32)
    same = np.eye(2)
    out = (amp * wave(step, -1.0)).reshape(ROWS, KC, NB)
    out = np.einsum("akj,pq->pjaqk", out, same).reshape(2 * NB, ROWS * 2 * KC)
    out = np.concatenate([out, out], axis=1)
    out = np.concatenate(halves(out), axis=0)
    back = (amp * wave(step + 1.0, 1.0)).reshape(ROWS, KC, NB)
    back = np.einsum("akj,pq->apkqj", back, same).reshape(ROWS * 2 * KC, 2 * NB)
    back = np.concatenate(halves(back), axis=1)
    last = wave(step, -1.0).reshape(ROWS // 2, 2, KC, NB // 2, 2)
    last = last.transpose(0, 4, 3, 1, 2)
    last = np.broadcast_to(last[:, :, :, :, None, :], last.shape[:4] + (PS, KC))
    last = last.reshape(ROWS * (NB // 2), 2 * PS * KC).astype(np.float32)
    return mix, out, back, last


def sine_terms():
    t = np.cos(np.pi * (np.arange(400) + 0.5) / 400) * 0.5
    t = t[t > 0]
    u = t * t
    basis = np.stack([u**n for n in range(5)], 1)
    return [float(v) for v in np.linalg.lstsq(basis, np.sin(np.pi * t) / t, rcond=None)[0]]


SINE = sine_terms()


def residue(x):
    q = (x.astype(F32) * (1.0 / PRIME)).astype(jnp.int32)
    r = x - q * PRIME
    r = jnp.where(r < 0, r + PRIME, r)
    return jnp.where(r >= PRIME, r - PRIME, r)


def place():
    r, c = lax.axis_index("row"), lax.axis_index("col")
    return (c // 4) * 4 + r // 8, c % 4, (r // 2) % 4, r % 2


def device(z, x, y, core):
    return ((z % 4) * 8 + y * 2 + core, (z // 4) * 4 + x)


def kernel(seeds, damp_hbm, mix_hbm, out_tab, back_tab, last_hbm, result,
           damp, mix, last, probes, fsend, xrecv, summed, mid, gsend, gbuf,
           hacc, hx, t4h, t4l, bsend, brecv, gz, gyc, gx,
           load_sem, xs_sem, xr_sem, us_sem, ur_sem, gs_sem, gr_sem, as_sem, ar_sem,
           hs_sem, hr_sem, bs_sem, br_sem, qs_sem, qr_sem):
    z, x, y, core = place()
    row, col = lax.axis_index("row"), lax.axis_index("col")
    here = z * 8 + y * 2 + core

    def there(t):
        return device(t // 8, x, (t // 2) % 4, t % 2)

    def beside(d):
        return device(z, (x + d) % NX, y, core)

    loads = [
        pltpu.make_async_copy(mix_hbm.at[pl.ds(pl.multiple_of(row * KC, KC), KC)], mix, load_sem.at[0]),
        pltpu.make_async_copy(damp_hbm, damp, load_sem.at[1]),
        pltpu.make_async_copy(last_hbm.at[pl.ds(pl.multiple_of(row * 16, 16), 16)], last, load_sem.at[2]),
    ]
    for load in loads:
        load.start()
    barrier = pltpu.get_barrier_semaphore()
    for d in range(1, NX):
        pl.semaphore_signal(barrier, inc=1, device_id=beside(d), device_id_type=MESH)

    @pl.loop(1, 64)
    def _(d):
        pl.semaphore_signal(barrier, inc=1, device_id=there((here + d) % 64), device_id_type=MESH)

    column = col * TILE + lax.broadcasted_iota(jnp.int32, (1, TILE), 1)
    pcol = lax.broadcasted_iota(jnp.int32, (PS, 1), 0)
    pone = (pcol + 1).astype(F32)

    @pl.loop(0, NB)
    def _(j):
        s = seeds[j]
        inner = residue(residue(s * (column + 1)) * (column + 3)).astype(F32)
        second = (residue(s * (pcol + 1)) * (pcol + 2)).astype(F32)
        phase = inner * pone + second
        phase = phase - jnp.floor(phase * (1.0 / PRIME) + 0.5) * PRIME
        t = phase * (1.0 / PRIME)
        u = t * t
        poly = SINE[4]
        for n in (3, 2, 1, 0):
            poly = poly * u + SINE[n]
        sine = poly * t
        probes[pl.ds(pl.multiple_of(j * PS, PS), PS), :] = (1.0 - 2.0 * sine * sine).astype(BF16)

    loads[0].wait()
    spread = jnp.broadcast_to(mix[...][None], (PS, KC, NB * PS)).reshape(PS * KC, NB * PS)
    r_idx = lax.broadcasted_iota(jnp.int32, (PS * KC, NB * PS), 0) // KC
    l_idx = lax.broadcasted_iota(jnp.int32, (PS * KC, NB * PS), 1) % PS
    spread = jnp.where(r_idx == l_idx, spread, 0.0).astype(BF16)
    terms = jnp.dot(spread, probes[...], preferred_element_type=F32).astype(BF16)
    wide = lax.broadcasted_iota(jnp.int32, (TILE, TILE * OWN), 1) // OWN
    tall = lax.broadcasted_iota(jnp.int32, (TILE, TILE * OWN), 0)
    expand = jnp.where(wide == tall, 1.0, 0.0).astype(BF16)
    k_row = (lax.broadcasted_iota(jnp.int32, (PS * KC, TILE * OWN), 0) % KC) // 2
    k_lane = lax.broadcasted_iota(jnp.int32, (PS * KC, TILE * OWN), 1) % OWN
    terms = jnp.dot(terms, expand, preferred_element_type=F32)
    terms = jnp.where(k_row == k_lane, terms, 0.0).astype(BF16)

    loads[1].wait()
    pl.semaphore_wait(barrier, 63 + NX - 1)
    sends = []
    for b in range(CHUNKS):
        part = damp[:, :, b * 512 : (b + 1) * 512].reshape(TILE * OWN, 512)
        got = jnp.dot(terms, part, preferred_element_type=F32).astype(BF16)
        for q in range(NX):
            fsend[b, q] = got[:, q * 128 : (q + 1) * 128]
        for d in (2, 1, 3):
            copy = pltpu.make_async_remote_copy(
                src_ref=fsend.at[b, (x + d) % NX], dst_ref=xrecv.at[b, d - 1],
                send_sem=xs_sem.at[b, d - 1], recv_sem=xr_sem.at[b, d - 1],
                device_id=beside(d), device_id_type=MESH)
            copy.start()
            sends.append(copy)

    loads[2].wait()
    same_p = (lax.broadcasted_iota(jnp.int32, (PS, 2 * PS * KC), 0)
              == (lax.broadcasted_iota(jnp.int32, (PS, 2 * PS * KC), 1) // KC) % PS)
    for jj in range(NB // 2):
        line = jnp.where(same_p, last[jj : jj + 1, :], 0.0)
        high = line.astype(BF16)
        t4h[jj * PS : (jj + 1) * PS, :] = high
        t4l[jj * PS : (jj + 1) * PS, :] = (line - high.astype(F32)).astype(BF16)

    for b in range(CHUNKS):
        total = fsend[b, x].astype(F32)
        for d in (1, 3, 2):
            sends[b * 3 + {2: 0, 1: 1, 3: 2}[d]].wait_recv()
            total = total + xrecv[b, d - 1].astype(F32)
        summed[b] = total.astype(BF16)

        @pl.loop(0, 16)
        def _(n):
            unit = (n + z * 2 + core) % 16
            src = summed.at[b, pl.ds(pl.multiple_of(unit * 16, 16), 16), :]
            mine = jnp.logical_and(n == 0, y == b)

            @pl.when(mine)
            def _():
                pltpu.make_async_copy(src, mid.at[here], ur_sem).start()

            @pl.when(jnp.logical_not(mine))
            def _():
                pltpu.make_async_remote_copy(
                    src_ref=src, dst_ref=mid.at[here], send_sem=us_sem, recv_sem=ur_sem,
                    device_id=device(unit // 2, x, b, unit % 2), device_id_type=MESH).start()

    @pl.when(y < CHUNKS)
    def _():
        pltpu.make_async_copy(mid, mid, ur_sem).wait()
        both = jnp.dot(out_tab[...], mid[...].reshape(1024, 128), preferred_element_type=F32)
        forward = (both[: 2 * NB] + both[2 * NB :]).astype(BF16)
        twice = jnp.concatenate([forward, forward], axis=0)
        gsend[...] = jnp.dot(back_tab[...], twice, preferred_element_type=F32).astype(BF16).reshape(ROWS, 16, 128)
        dst = gbuf.at[pl.ds(pl.multiple_of((z * 2 + core) * 16, 16), 16),
                      pl.ds(pl.multiple_of((y * NX + x) * 128, 128), 128)]
        pltpu.make_async_copy(gsend.at[row], dst, gr_sem.at[y]).start()

        @pl.loop(1, 64)
        def _(d):
            t = (here + d) % 64
            pltpu.make_async_remote_copy(
                src_ref=gsend.at[t % 32], dst_ref=dst, send_sem=gs_sem, recv_sem=gr_sem.at[y],
                device_id=there(t), device_id_type=MESH).start()

    gathers = []
    for b in range(CHUNKS):
        block = gbuf.at[:, pl.ds(pl.multiple_of((b * NX + x) * 128, 128), 128)]
        pltpu.make_async_copy(block, block, gr_sem.at[b]).wait()
        for d in (2, 1, 3):
            copy = pltpu.make_async_remote_copy(
                src_ref=block, dst_ref=block, send_sem=as_sem.at[b, d - 1], recv_sem=ar_sem.at[b, d - 1],
                device_id=beside(d), device_id_type=MESH)
            copy.start()
            gathers.append(copy)
    for b in range(CHUNKS):
        for copy in gathers[b * 3 : b * 3 + 3]:
            copy.wait_recv()
        part = damp[:, :, b * 512 : (b + 1) * 512].reshape(TILE * OWN, 512)
        got = lax.dot_general(gbuf[:, b * 512 : (b + 1) * 512], part, (((1,), (1,)), ((), ())),
                              preferred_element_type=F32)
        hacc[...] = got if b == 0 else hacc[...] + got
    back = jnp.where(k_row == k_lane, hacc[...], 0.0).astype(BF16)
    back = lax.dot_general(back, expand, (((1,), (1,)), ((), ())), preferred_element_type=F32).astype(BF16)
    hx[core] = back
    swap = pltpu.make_async_remote_copy(
        src_ref=hx.at[core], dst_ref=hx.at[core], send_sem=hs_sem, recv_sem=hr_sem,
        device_id=device(z, x, y, 1 - core), device_id_type=MESH)
    swap.start()
    swap.wait()

    pair = hx[...].reshape(2 * PS * KC, TILE)
    blocks = jnp.dot(t4h[...], pair, preferred_element_type=F32)
    blocks = blocks + jnp.dot(t4l[...], pair, preferred_element_type=F32)
    bsend[...] = blocks.astype(BF16).reshape(16, PS, TILE)
    chip = (z % 4) * 4 + y
    pltpu.make_async_copy(bsend.at[chip], brecv.at[chip], br_sem).start()

    @pl.loop(1, 16)
    def _(d):
        t = (chip + d) % 16
        pltpu.make_async_remote_copy(
            src_ref=bsend.at[t], dst_ref=brecv.at[chip], send_sem=bs_sem, recv_sem=br_sem,
            device_id=device((z // 4) * 4 + t // 4, x, t % 4, core), device_id_type=MESH).start()

    pltpu.make_async_copy(brecv, brecv, br_sem).wait()
    mine = jnp.sum(brecv[...].astype(F32), axis=0)

    gram = lax.dot_general(mine, mine, (((1,), (1,)), ((), ())), precision=HIGHEST, preferred_element_type=F32)
    gram = jnp.concatenate([gram[n * 8 : n * 8 + 8] for n in range(4)], axis=1)
    for stage, (buf, number, me, who) in enumerate((
        (gz, 8, z, lambda t: device(t, x, y, core)),
        (gyc, 8, y * 2 + core, lambda t: device(z, x, t // 2, t % 2)),
        (gx, 4, x, lambda t: device(z, t, y, core)),
    )):
        buf[me] = gram
        for d in range(1, number):
            pltpu.make_async_remote_copy(
                src_ref=buf.at[me], dst_ref=buf.at[me], send_sem=qs_sem.at[stage], recv_sem=qr_sem.at[stage],
                device_id=who((me + d) % number), device_id_type=MESH).start()
        some = buf.at[pl.ds(0, number - 1)]
        pltpu.make_async_copy(some, some, qr_sem.at[stage]).wait()
        pltpu.make_async_copy(some, some, qs_sem.at[stage]).wait()
        gram = jnp.sum(buf[...], axis=0)
    gram = jnp.concatenate([gram[:, n * 32 : n * 32 + 32] for n in range(4)], axis=0)

    eye = jnp.where(lax.broadcasted_iota(jnp.int32, (PS, PS), 0) == lax.broadcasted_iota(jnp.int32, (PS, PS), 1), 1.0, 0.0)
    scale = jnp.sum(gram * eye, keepdims=True) + 1e-06
    current = gram / scale
    inverse = eye
    for _ in range(NSTEPS):
        weight = 1.5 * eye - 0.5 * jnp.dot(inverse, current, precision=HIGHEST, preferred_element_type=F32)
        current = jnp.dot(current, weight, precision=HIGHEST, preferred_element_type=F32)
        inverse = jnp.dot(weight, inverse, precision=HIGHEST, preferred_element_type=F32)
    answer = lax.dot_general(inverse, mine, (((0,), (0,)), ((), ())), precision=HIGHEST, preferred_element_type=F32)
    result[...] = answer * (math.sqrt(NB * M) / jnp.sqrt(scale))

    for copy in sends + gathers:
        copy.wait_send()
    rest = bsend.at[pl.ds(0, 15)]
    pltpu.make_async_copy(rest, rest, bs_sem).wait()

    @pl.when(y < CHUNKS)
    def _():
        most = mid.at[pl.ds(0, 47)]
        pltpu.make_async_copy(most, most, us_sem).wait()
        most = mid.at[pl.ds(0, 63)]
        pltpu.make_async_copy(most, most, gs_sem).wait()

    @pl.when(y >= CHUNKS)
    def _():
        most = mid.at[pl.ds(0, 48)]
        pltpu.make_async_copy(most, most, us_sem).wait()


def shards(damping, block_seeds):
    mix, out, back, last = tables()
    vmem, anywhere = pl.BlockSpec(memory_space=pltpu.VMEM), pl.BlockSpec(memory_space=pl.ANY)
    dma = pltpu.SemaphoreType.DMA
    turned = pl.pallas_call(
        kernel,
        out_shape=jax.ShapeDtypeStruct((PS, TILE), F32),
        in_specs=[pl.BlockSpec(memory_space=pltpu.SMEM), anywhere, anywhere, vmem, vmem, anywhere],
        out_specs=vmem,
        scratch_shapes=[
            pltpu.VMEM((TILE, OWN, M), BF16),
            pltpu.VMEM((KC, NB * PS), F32),
            pltpu.VMEM((16, 2 * PS * KC), F32),
            pltpu.VMEM((NB * PS, TILE), BF16),
            pltpu.VMEM((CHUNKS, NX, PS * KC, 128), BF16),
            pltpu.VMEM((CHUNKS, NX - 1, PS * KC, 128), BF16),
            pltpu.VMEM((CHUNKS, PS * KC, 128), BF16),
            pltpu.VMEM((64, 16, 128), BF16),
            pltpu.VMEM((ROWS, 16, 128), BF16),
            pltpu.VMEM((PS * KC, M), BF16),
            pltpu.VMEM((PS * KC, TILE * OWN), F32),
            pltpu.VMEM((2, PS * KC, TILE), BF16),
            pltpu.VMEM((512, 512), BF16),
            pltpu.VMEM((512, 512), BF16),
            pltpu.VMEM((16, PS, TILE), BF16),
            pltpu.VMEM((16, PS, TILE), BF16),
            pltpu.VMEM((8, 8, 128), F32),
            pltpu.VMEM((8, 8, 128), F32),
            pltpu.VMEM((4, 8, 128), F32),
            dma((3,)), dma((CHUNKS, 3)), dma((CHUNKS, 3)), dma, dma, dma, dma((CHUNKS,)),
            dma((CHUNKS, 3)), dma((CHUNKS, 3)), dma, dma, dma, dma, dma((3,)), dma((3,)),
        ],
        compiler_params=pltpu.CompilerParams(
            collective_id=0, has_side_effects=True, vmem_limit_bytes=48 << 20),
        name="hankel",
    )(block_seeds, damping, jnp.asarray(mix), jnp.asarray(out), jnp.asarray(back), jnp.asarray(last))
    return turned.T[None]


def solution(mesh):
    return jax.shard_map(
        shards,
        mesh=mesh,
        in_specs=(P("col", "row", None), P()),
        out_specs=P("row", "col", None),
        check_vma=False,
    )
```

```python
import functools
import math

import jax
import jax.numpy as jnp
import numpy as np
from jax import lax
from jax.experimental import pallas as pl
from jax.experimental.pallas import tpu as pltpu
from jax.sharding import PartitionSpec as P

NF = 128
M = 1536
PS = 32
NB = 32
NSTEPS = 12
PRIME = 65521
OWN = 4
KC = 2 * OWN
ROWS = 32
TILE = 192
NX, NY, NZ = 4, 4, 8
CHUNKS = 3
MESH = pl.DeviceIdType.MESH
F32, BF16 = jnp.float32, jnp.bfloat16
HIGHEST = lax.Precision.HIGHEST


def wave(step, sign):
    freq = np.arange(NF)[:, None] + 0.5
    angle = math.pi * freq * step[None, :] / NF
    window = np.exp(-math.log(3.0) * step / NB)[None, :]
    return np.stack([np.cos(angle) * window, sign * np.sin(angle) * window], 1).reshape(2 * NF, len(step))


def halves(table):
    high = table.astype(jnp.bfloat16)
    low = (table - high.astype(np.float64)).astype(jnp.bfloat16)
    return high, low


def tables():
    step = np.arange(NB).astype(np.float64)
    amp = math.sqrt(2.0 / NF) / math.sqrt(NB * M)
    mix = np.repeat(wave(step, 1.0), PS, axis=1).astype(np.float32)
    same = np.eye(2)
    out = (amp * wave(step, -1.0)).reshape(ROWS, KC, NB)
    out = np.einsum("akj,pq->pjaqk", out, same).reshape(2 * NB, ROWS * 2 * KC)
    out = np.concatenate([out, out], axis=1)
    out = np.concatenate(halves(out), axis=0)
    back = (amp * wave(step + 1.0, 1.0)).reshape(ROWS, KC, NB)
    back = np.einsum("akj,pq->apkqj", back, same).reshape(ROWS * 2 * KC, 2 * NB)
    back = np.concatenate(halves(back), axis=1)
    last = wave(step, -1.0).reshape(ROWS // 2, 2, KC, NB // 2, 2)
    last = last.transpose(0, 4, 3, 1, 2)
    last = np.broadcast_to(last[:, :, :, :, None, :], last.shape[:4] + (PS, KC))
    last = last.reshape(ROWS * (NB // 2), 2 * PS * KC).astype(np.float32)
    return mix, out, back, last


def sine_terms():
    t = np.cos(np.pi * (np.arange(400) + 0.5) / 400) * 0.5
    t = t[t > 0]
    u = t * t
    basis = np.stack([u**n for n in range(5)], 1)
    return [float(v) for v in np.linalg.lstsq(basis, np.sin(np.pi * t) / t, rcond=None)[0]]


SINE = sine_terms()


def residue(x):
    q = (x.astype(F32) * (1.0 / PRIME)).astype(jnp.int32)
    r = x - q * PRIME
    r = jnp.where(r < 0, r + PRIME, r)
    return jnp.where(r >= PRIME, r - PRIME, r)


def place():
    r, c = lax.axis_index("row"), lax.axis_index("col")
    return (c // 4) * 4 + r // 8, c % 4, (r // 2) % 4, r % 2


def device(z, x, y, core):
    return ((z % 4) * 8 + y * 2 + core, (z // 4) * 4 + x)


def kernel(seeds, damp_hbm, mix_hbm, out_hbm, back_hbm, last_hbm, result,
           damp, mix, last, out_tab, back_tab, probes, fsend, xrecv, summed, mid, gsend, gbuf,
           hacc, hx, t4h, t4l, bsend, brecv, gz, gx,
           load_sem, xs_sem, xr_sem, us_sem, ur_sem, gs_sem, gr_sem, as_sem, ar_sem,
           hs_sem, hr_sem, bs_sem, br_sem, qs_sem, qr_sem):
    z, x, y, core = place()
    row, col = lax.axis_index("row"), lax.axis_index("col")
    here = z * 8 + y * 2 + core
    turn = (y + 8 - z) % NY

    def there(t):
        return device(t // 8, x, (t // 2) % 4, t % 2)

    def beside(d):
        return device(z, (x + d) % NX, y, core)

    loads = [
        pltpu.make_async_copy(mix_hbm.at[pl.ds(pl.multiple_of(row * KC, KC), KC)], mix, load_sem.at[0]),
        pltpu.make_async_copy(damp_hbm, damp, load_sem.at[1]),
        pltpu.make_async_copy(last_hbm.at[pl.ds(pl.multiple_of(row * 16, 16), 16)], last, load_sem.at[2]),
        pltpu.make_async_copy(out_hbm, out_tab, load_sem.at[3]),
        pltpu.make_async_copy(back_hbm, back_tab, load_sem.at[4]),
    ]
    for load in loads:
        load.start()
    barrier = pltpu.get_barrier_semaphore()

    @pl.loop(0, 16)
    def _(d):
        @pl.when(d % NX > 0)
        def _():
            pl.semaphore_signal(barrier, inc=1, device_id=device(z, (x + d) % NX, (y + d // NX) % NY, core),
                                device_id_type=MESH)

    @pl.loop(1, 64)
    def _(d):
        pl.semaphore_signal(barrier, inc=1, device_id=there((here + d) % 64), device_id_type=MESH)

    column = col * TILE + lax.broadcasted_iota(jnp.int32, (1, TILE), 1)
    pcol = lax.broadcasted_iota(jnp.int32, (PS, 1), 0)
    pone = (pcol + 1).astype(F32)

    @pl.loop(0, NB)
    def _(j):
        s = seeds[j]
        inner = residue(residue(s * (column + 1)) * (column + 3)).astype(F32)
        second = (residue(s * (pcol + 1)) * (pcol + 2)).astype(F32)
        phase = inner * pone + second
        phase = phase - jnp.floor(phase * (1.0 / PRIME) + 0.5) * PRIME
        t = phase * (1.0 / PRIME)
        u = t * t
        poly = SINE[4]
        for n in (3, 2, 1, 0):
            poly = poly * u + SINE[n]
        sine = poly * t
        probes[pl.ds(pl.multiple_of(j * PS, PS), PS), :] = (1.0 - 2.0 * sine * sine).astype(BF16)

    loads[0].wait()
    spread = jnp.broadcast_to(mix[...][None], (PS, KC, NB * PS)).reshape(PS * KC, NB * PS)
    r_idx = lax.broadcasted_iota(jnp.int32, (PS * KC, NB * PS), 0) // KC
    l_idx = lax.broadcasted_iota(jnp.int32, (PS * KC, NB * PS), 1) % PS
    spread = jnp.where(r_idx == l_idx, spread, 0.0).astype(BF16)
    terms = jnp.dot(spread, probes[...], preferred_element_type=F32).astype(BF16)
    wide = lax.broadcasted_iota(jnp.int32, (TILE, TILE * OWN), 1) // OWN
    tall = lax.broadcasted_iota(jnp.int32, (TILE, TILE * OWN), 0)
    expand = jnp.where(wide == tall, 1.0, 0.0).astype(BF16)
    k_row = (lax.broadcasted_iota(jnp.int32, (PS * KC, TILE * OWN), 0) % KC) // 2
    k_lane = lax.broadcasted_iota(jnp.int32, (PS * KC, TILE * OWN), 1) % OWN
    terms = jnp.dot(terms, expand, preferred_element_type=F32)
    terms = jnp.where(k_row == k_lane, terms, 0.0).astype(BF16)

    loads[1].wait()
    pl.semaphore_wait(barrier, 63 + 12)
    sends = []
    for b in range(CHUNKS):
        part = damp[:, :, b * 512 : (b + 1) * 512].reshape(TILE * OWN, 512)
        got = jnp.dot(terms, part, preferred_element_type=F32).astype(BF16)
        for q in range(NX):
            fsend[b, q] = got[:, q * 128 : (q + 1) * 128]
        for d in (2, 1, 3):
            copy = pltpu.make_async_remote_copy(
                src_ref=fsend.at[b, (x + d) % NX], dst_ref=xrecv.at[b, d - 1],
                send_sem=xs_sem.at[b, d - 1], recv_sem=xr_sem.at[b, d - 1],
                device_id=beside(d), device_id_type=MESH)
            copy.start()
            sends.append(copy)

    for load in loads[2:]:
        load.wait()
    p_lane = (lax.broadcasted_iota(jnp.int32, (PS, 2 * PS * KC), 1) // KC) % PS
    p_row = lax.broadcasted_iota(jnp.int32, (PS, 2 * PS * KC), 0)
    for jj in range(NB // 2):
        line = jnp.broadcast_to(last[jj : jj + 1, :], (PS, 2 * PS * KC))
        high = line.astype(BF16).astype(F32)
        for keep, rows, at in ((p_row == p_lane, PS, 0), ((p_row == p_lane % 16)[:16], 16, 512)):
            out = pl.ds(at + jj * rows, rows)
            t4h[out, :] = jnp.where(keep, high[:rows], 0.0).astype(BF16)
            t4l[out, :] = jnp.where(keep, (line - high)[:rows], 0.0).astype(BF16)
    for b in range(CHUNKS):
        total = fsend[b, x].astype(F32)
        for d in (1, 3, 2):
            sends[b * 3 + {2: 0, 1: 1, 3: 2}[d]].wait_recv()
            total = total + xrecv[b, d - 1].astype(F32)
        summed[b] = total.astype(BF16)

        @pl.loop(0, 16)
        def _(n):
            unit = (n + z * 2 + core) % 16
            src = summed.at[b, pl.ds(pl.multiple_of(unit * 16, 16), 16), :]
            mine = jnp.logical_and(n == 0, turn == b)

            @pl.when(mine)
            def _():
                pltpu.make_async_copy(src, mid.at[here], ur_sem).start()

            @pl.when(jnp.logical_not(mine))
            def _():
                pltpu.make_async_remote_copy(
                    src_ref=src, dst_ref=mid.at[here], send_sem=us_sem, recv_sem=ur_sem,
                    device_id=device(unit // 2, x, (b + unit // 2) % NY, unit % 2), device_id_type=MESH).start()

    @pl.when(turn < CHUNKS)
    def _():
        pltpu.make_async_copy(mid, mid, ur_sem).wait()
        both = jnp.dot(out_tab[...], mid[...].reshape(1024, 128), preferred_element_type=F32)
        forward = (both[: 2 * NB] + both[2 * NB :]).astype(BF16)
        twice = jnp.concatenate([forward, forward], axis=0)
        gsend[...] = jnp.dot(back_tab[...], twice, preferred_element_type=F32).astype(BF16).reshape(ROWS, 16, 128)
        dst = gbuf.at[pl.ds(pl.multiple_of((z * 2 + core) * 16, 16), 16),
                      pl.ds(pl.multiple_of((turn * NX + x) * 128, 128), 128)]
        pltpu.make_async_copy(gsend.at[row], dst, gr_sem.at[turn]).start()

        @pl.loop(1, 64)
        def _(d):
            t = (here + d) % 64
            pltpu.make_async_remote_copy(
                src_ref=gsend.at[t % 32], dst_ref=dst, send_sem=gs_sem, recv_sem=gr_sem.at[turn],
                device_id=there(t), device_id_type=MESH).start()

    gathers = []
    for b in range(CHUNKS):
        block = gbuf.at[:, pl.ds(pl.multiple_of((b * NX + x) * 128, 128), 128)]
        pltpu.make_async_copy(block, block, gr_sem.at[b]).wait()
        for d in (2, 1, 3):
            copy = pltpu.make_async_remote_copy(
                src_ref=block, dst_ref=block, send_sem=as_sem.at[b, d - 1], recv_sem=ar_sem.at[b, d - 1],
                device_id=beside(d), device_id_type=MESH)
            copy.start()
            gathers.append(copy)
    for b in range(CHUNKS):
        for copy in gathers[b * 3 : b * 3 + 3]:
            copy.wait_recv()
        part = damp[:, :, b * 512 : (b + 1) * 512].reshape(TILE * OWN, 512)
        got = lax.dot_general(gbuf[:, b * 512 : (b + 1) * 512], part, (((1,), (1,)), ((), ())),
                              preferred_element_type=F32)
        hacc[...] = got if b == 0 else hacc[...] + got
    back = jnp.where(k_row == k_lane, hacc[...], 0.0).astype(BF16)
    fold = jnp.concatenate([expand, expand[128:]], axis=0)
    back = lax.dot_general(back, fold, (((1,), (1,)), ((), ())), preferred_element_type=F32)
    upper = lax.broadcasted_iota(jnp.int32, (PS * KC, 256), 0) >= PS * KC // 2
    lane = lax.broadcasted_iota(jnp.int32, (PS * KC, 256), 1)
    back = jnp.where(jnp.logical_or(lane < 128, upper == (lane >= TILE)), back, 0.0).astype(BF16)
    hx[core] = back
    swap = pltpu.make_async_remote_copy(
        src_ref=hx.at[core], dst_ref=hx.at[core], send_sem=hs_sem, recv_sem=hr_sem,
        device_id=device(z, x, y, 1 - core), device_id_type=MESH)
    swap.start()
    swap.wait()

    for rows, at, to, lanes in ((PS, 0, 0, 0), (16, 512, PS, 128)):
        pair = hx[:, :, lanes : lanes + 128].reshape(2 * PS * KC, 128)
        blocks = jnp.dot(t4h[at : at + 16 * rows, :], pair, preferred_element_type=F32)
        blocks = blocks + jnp.dot(t4l[at : at + 16 * rows, :], pair, preferred_element_type=F32)
        bsend[:, to : to + rows, :] = blocks.astype(BF16).reshape(16, rows, 128)
    chip = (z % 4) * 4 + y
    pltpu.make_async_copy(bsend.at[chip], brecv.at[chip], br_sem).start()

    @pl.loop(1, 16)
    def _(d):
        t = (chip + d) % 16
        pltpu.make_async_remote_copy(
            src_ref=bsend.at[t], dst_ref=brecv.at[chip], send_sem=bs_sem, recv_sem=br_sem,
            device_id=device((z // 4) * 4 + t // 4, x, t % 4, core), device_id_type=MESH).start()

    pltpu.make_async_copy(brecv, brecv, br_sem).wait()
    mine = jnp.sum(brecv[...].astype(F32), axis=0)
    edge = mine[PS:]
    low = lax.broadcasted_iota(jnp.int32, (16, 128), 1) < 64
    edge = jnp.concatenate([jnp.where(low, edge, 0.0), jnp.where(low, pltpu.roll(edge, 64, 1), 0.0)], axis=0)
    mine = jnp.concatenate([mine[:PS], edge], axis=1)

    group = lax.broadcasted_iota(jnp.int32, (8, 128), 1) // PS
    gram = lax.dot_general(mine, jnp.concatenate([mine] * 4, axis=0), (((1,), (1,)), ((), ())),
                           precision=HIGHEST, preferred_element_type=F32)
    packed = gram[0:8]
    for n in range(1, 4):
        packed = jnp.where(group == n, gram[n * 8 : n * 8 + 8], packed)
    for stage, (buf, me, who) in enumerate((
        (gz, z * 2 + core, lambda t: device(t // 2, x, y, t % 2)),
        (gx, x * 4 + y, lambda t: device(z, t // 4, t % 4, core)),
    )):
        buf[me] = packed

        @pl.loop(1, 16)
        def _(d):
            pltpu.make_async_remote_copy(
                src_ref=buf.at[me], dst_ref=buf.at[me], send_sem=qs_sem.at[stage], recv_sem=qr_sem.at[stage],
                device_id=who((me + d) % 16), device_id_type=MESH).start()
        some = buf.at[pl.ds(0, 15)]
        pltpu.make_async_copy(some, some, qr_sem.at[stage]).wait()
        pltpu.make_async_copy(some, some, qs_sem.at[stage]).wait()
        packed = jnp.sum(buf[...], axis=0)

    turned = [packed] + [pltpu.roll(packed, n * PS, 1) for n in range(1, 4)]
    strips = []
    for n in range(4):
        strip = turned[(4 - n) % 4]
        for g in range(1, 4):
            strip = jnp.where(group == g, turned[(g - n) % 4], strip)
        strips.append(strip)
    gram = jnp.concatenate(strips, axis=0)
    s_row = lax.broadcasted_iota(jnp.int32, (PS, 128), 0)
    s_lane = lax.broadcasted_iota(jnp.int32, (PS, 128), 1)
    eye = jnp.where(s_row == s_lane % PS, 1.0, 0.0)
    scale = jnp.sum(jnp.where(s_row == s_lane, gram, 0.0), keepdims=True) + 1e-06

    def left(a):
        high = a.astype(BF16).astype(F32)
        lane = lax.broadcasted_iota(jnp.int32, a.shape, 1)
        return jnp.where(lane < 64, high, a - high).astype(BF16)

    def right(a):
        high = a.astype(BF16)
        low = (a - high.astype(F32)).astype(BF16)
        return jnp.concatenate([high, low, high, low], axis=0)

    square = gram / scale
    inverse = eye
    for step in range(NSTEPS):
        weight = 1.5 * eye - 0.5 * square
        factor = right(weight)
        both = jnp.dot(left(jnp.concatenate([square, inverse], axis=0)), factor, preferred_element_type=F32)
        inverse = both[PS:]
        if step < NSTEPS - 1:
            square = jnp.dot(left(both[:PS]), factor, preferred_element_type=F32)
    answer = jnp.dot(left(inverse), right(mine), preferred_element_type=F32)
    result[...] = answer[:, :TILE] * (math.sqrt(NB * M) / jnp.sqrt(scale))

    for copy in sends + gathers:
        copy.wait_send()
    rest = bsend.at[pl.ds(0, 15)]
    pltpu.make_async_copy(rest, rest, bs_sem).wait()

    @pl.when(turn < CHUNKS)
    def _():
        most = mid.at[pl.ds(0, 47)]
        pltpu.make_async_copy(most, most, us_sem).wait()
        most = mid.at[pl.ds(0, 63)]
        pltpu.make_async_copy(most, most, gs_sem).wait()

    @pl.when(turn >= CHUNKS)
    def _():
        most = mid.at[pl.ds(0, 48)]
        pltpu.make_async_copy(most, most, us_sem).wait()


def shards(damping, block_seeds):
    mix, out, back, last = tables()
    vmem, anywhere = pl.BlockSpec(memory_space=pltpu.VMEM), pl.BlockSpec(memory_space=pl.ANY)
    dma = pltpu.SemaphoreType.DMA
    turned = pl.pallas_call(
        kernel,
        out_shape=jax.ShapeDtypeStruct((PS, TILE), F32),
        in_specs=[pl.BlockSpec(memory_space=pltpu.SMEM), anywhere, anywhere, anywhere, anywhere, anywhere],
        out_specs=vmem,
        scratch_shapes=[
            pltpu.VMEM((TILE, OWN, M), BF16),
            pltpu.VMEM((KC, NB * PS), F32),
            pltpu.VMEM((16, 2 * PS * KC), F32),
            pltpu.VMEM((4 * NB, 1024), BF16),
            pltpu.VMEM((512, 4 * NB), BF16),
            pltpu.VMEM((NB * PS, TILE), BF16),
            pltpu.VMEM((CHUNKS, NX, PS * KC, 128), BF16),
            pltpu.VMEM((CHUNKS, NX - 1, PS * KC, 128), BF16),
            pltpu.VMEM((CHUNKS, PS * KC, 128), BF16),
            pltpu.VMEM((64, 16, 128), BF16),
            pltpu.VMEM((ROWS, 16, 128), BF16),
            pltpu.VMEM((PS * KC, M), BF16),
            pltpu.VMEM((PS * KC, TILE * OWN), F32),
            pltpu.VMEM((2, PS * KC, 256), BF16),
            pltpu.VMEM((768, 512), BF16),
            pltpu.VMEM((768, 512), BF16),
            pltpu.VMEM((16, 48, 128), BF16),
            pltpu.VMEM((16, 48, 128), BF16),
            pltpu.VMEM((16, 8, 128), F32),
            pltpu.VMEM((16, 8, 128), F32),
            dma((5,)), dma((CHUNKS, 3)), dma((CHUNKS, 3)), dma, dma, dma, dma((CHUNKS,)),
            dma((CHUNKS, 3)), dma((CHUNKS, 3)), dma, dma, dma, dma, dma((2,)), dma((2,)),
        ],
        compiler_params=pltpu.CompilerParams(
            collective_id=0, has_side_effects=True, vmem_limit_bytes=62 << 20),
        name="hankel",
    )(block_seeds, damping, jnp.asarray(mix), jnp.asarray(out), jnp.asarray(back), jnp.asarray(last))
    return turned.T[None]


def solution(mesh):
    return jax.shard_map(
        shards,
        mesh=mesh,
        in_specs=(P("col", "row", None), P()),
        out_specs=P("row", "col", None),
        check_vma=False,
    )
```

```python
import functools
import math

import jax
import jax.numpy as jnp
import numpy as np
from jax import lax
from jax.experimental import pallas as pl
from jax.experimental.pallas import tpu as pltpu
from jax.sharding import PartitionSpec as P

NF = 128
M = 1536
PS = 32
NB = 32
NSTEPS = 12
PRIME = 65521
OWN = 4
KC = 2 * OWN
ROWS = 32
TILE = 192
NX, NY, NZ = 4, 4, 8
CHUNKS = 4
PC = PS // CHUNKS
CR = PC * KC
BLOCKS = 3
STRIP = BLOCKS * 128
MESH = pl.DeviceIdType.MESH
F32, BF16 = jnp.float32, jnp.bfloat16
HIGHEST = lax.Precision.HIGHEST


def wave(step, sign):
    freq = np.arange(NF)[:, None] + 0.5
    angle = math.pi * freq * step[None, :] / NF
    window = np.exp(-math.log(3.0) * step / NB)[None, :]
    return np.stack([np.cos(angle) * window, sign * np.sin(angle) * window], 1).reshape(2 * NF, len(step))


def halves(table):
    high = table.astype(jnp.bfloat16)
    low = (table - high.astype(np.float64)).astype(jnp.bfloat16)
    return high, low


def tables():
    step = np.arange(NB).astype(np.float64)
    amp = math.sqrt(2.0 / NF) / math.sqrt(NB * M)
    mix = np.repeat(wave(step, 1.0), PS, axis=1).astype(np.float32)
    same = np.eye(2)
    out = (amp * wave(step, -1.0)).reshape(ROWS, KC, NB)
    out = np.einsum("akj,pq->pjaqk", out, same).reshape(2 * NB, ROWS * 2 * KC)
    out = np.concatenate([out, out], axis=1)
    out = np.concatenate(halves(out), axis=0)
    back = (amp * wave(step + 1.0, 1.0)).reshape(ROWS, KC, NB)
    back = np.einsum("akj,pq->apkqj", back, same).reshape(ROWS * 2 * KC, 2 * NB)
    back = np.concatenate(halves(back), axis=1)
    last = wave(step, -1.0).reshape(ROWS // 2, 2, KC, NB // 2, 2)
    last = last.transpose(0, 4, 3, 1, 2)
    last = np.broadcast_to(last[:, :, :, :, None, :], last.shape[:4] + (PC, KC))
    last = last.reshape(ROWS * (NB // 2), 2 * CR).astype(np.float32)
    return mix, out, back, last


def sine_terms():
    t = np.cos(np.pi * (np.arange(400) + 0.5) / 400) * 0.5
    t = t[t > 0]
    u = t * t
    basis = np.stack([u**n for n in range(5)], 1)
    return [float(v) for v in np.linalg.lstsq(basis, np.sin(np.pi * t) / t, rcond=None)[0]]


SINE = sine_terms()


def residue(x):
    q = (x.astype(F32) * (1.0 / PRIME)).astype(jnp.int32)
    r = x - q * PRIME
    r = jnp.where(r < 0, r + PRIME, r)
    return jnp.where(r >= PRIME, r - PRIME, r)


FAR4 = (2, 1, 3, 0)
FAR8 = (4, 3, 5, 2, 6, 1, 7, 0)


def rem(a, n):
    return lax.rem(a, jnp.int32(n))


def div(a, n):
    return lax.div(a, jnp.int32(n))


def far8(k):
    half = div(k + 1, 2)
    return 4 + half - 2 * half * rem(k, 2)


def place():
    r, c = lax.axis_index("row"), lax.axis_index("col")
    return div(c, 4) * 4 + div(r, 8), rem(c, 4), rem(div(r, 2), 4), rem(r, 2)


def device(z, x, y, core):
    return (rem(z, 4) * 8 + y * 2 + core, div(z, 4) * 4 + x)


def kernel(seeds, damp_hbm, mix_hbm, out_hbm, back_hbm, last_hbm, result,
           damp, flat, mix, last, out_tab, back_tab, probes, fsend, xrecv, summed, mid, gsend, gbuf,
           hx, bsend, brecv, gz, gx,
           ready, load_sem, xs_sem, xr_sem, us_sem, ur_sem, gs_sem, gr_sem, as_sem, ar_sem,
           hs_sem, hr_sem, bs_sem, br_sem, qs_sem, qr_sem):
    z, x, y, core = place()
    row, col = lax.axis_index("row"), lax.axis_index("col")
    here = z * 8 + y * 2 + core
    my_chunk, my_pair, my_block = core * 2 + rem(z, 2), div(z, 2), rem(y + 4 - div(z, 2), NY)

    def beside(d):
        return device(z, rem(x + d, NX), y, core)

    def plane(dy, dc):
        return device(z, x, rem(y + dy, NY), core if dc == 0 else 1 - core)

    around = [(dy, dc) for dy in FAR4 for dc in (1, 0) if dy or dc]

    loads = [
        pltpu.make_async_copy(damp_hbm, damp, load_sem.at[1]),
        pltpu.make_async_copy(mix_hbm.at[pl.ds(pl.multiple_of(row * KC, KC), KC)], mix, load_sem.at[0]),
        pltpu.make_async_copy(last_hbm.at[pl.ds(pl.multiple_of(row * 16, 16), 16)], last, load_sem.at[2]),
        pltpu.make_async_copy(out_hbm, out_tab, load_sem.at[3]),
        pltpu.make_async_copy(back_hbm, back_tab, load_sem.at[4]),
    ]
    barrier = pltpu.get_barrier_semaphore()
    for d in FAR8[:-1]:
        pl.semaphore_signal(barrier, inc=1, device_id=device(rem(z + d, NZ), x, y, core), device_id_type=MESH)
    for dy, dc in around:
        pl.semaphore_signal(barrier, inc=1, device_id=plane(dy, dc), device_id_type=MESH)
    for d in FAR4[:-1]:
        pl.semaphore_signal(barrier, inc=1, device_id=beside(d), device_id_type=MESH)
    for load in loads:
        load.start()

    column = col * TILE + lax.broadcasted_iota(jnp.int32, (1, TILE), 1)
    pcol = lax.broadcasted_iota(jnp.int32, (PS, 1), 0)
    pone = (pcol + 1).astype(F32)

    @pl.loop(0, NB)
    def _(j):
        s = seeds[j]
        inner = residue(residue(s * (column + 1)) * (column + 3)).astype(F32)
        second = (residue(s * (pcol + 1)) * (pcol + 2)).astype(F32)
        phase = inner * pone + second
        phase = phase - jnp.floor(phase * (1.0 / PRIME) + 0.5) * PRIME
        t = phase * (1.0 / PRIME)
        u = t * t
        poly = SINE[4]
        for n in (3, 2, 1, 0):
            poly = poly * u + SINE[n]
        sine = poly * t
        probes[pl.ds(pl.multiple_of(j * PS, PS), PS), :] = (1.0 - 2.0 * sine * sine).astype(BF16)

    loads[1].wait()
    spread = jnp.broadcast_to(mix[...][None], (PS, KC, NB * PS)).reshape(PS * KC, NB * PS)
    r_idx = lax.broadcasted_iota(jnp.int32, (PS * KC, NB * PS), 0) // KC
    l_idx = lax.broadcasted_iota(jnp.int32, (PS * KC, NB * PS), 1) % PS
    spread = jnp.where(r_idx == l_idx, spread, 0.0).astype(BF16)
    terms = jnp.dot(spread, probes[...], preferred_element_type=F32).astype(BF16)
    wide = lax.broadcasted_iota(jnp.int32, (TILE, TILE * OWN), 1) // OWN
    tall = lax.broadcasted_iota(jnp.int32, (TILE, TILE * OWN), 0)
    expand = jnp.where(wide == tall, 1.0, 0.0).astype(BF16)
    k_row = (lax.broadcasted_iota(jnp.int32, (PS * KC, TILE * OWN), 0) % KC) // 2
    k_lane = lax.broadcasted_iota(jnp.int32, (PS * KC, TILE * OWN), 1) % OWN
    terms = jnp.dot(terms, expand, preferred_element_type=F32)
    terms = jnp.where(k_row == k_lane, terms, 0.0).astype(BF16)

    loads[0].wait()
    for n in range(3):
        flat[:, n * 512 : (n + 1) * 512] = damp[:, :, n * 512 : (n + 1) * 512].reshape(TILE * OWN, 512)
    for load in loads[2:]:
        load.wait()
    sends = []
    for b in range(CHUNKS):
        got = jnp.dot(terms[b * CR : (b + 1) * CR], flat[...], preferred_element_type=F32).astype(BF16)
        for q in range(NX):
            fsend[b, q] = got[:, q * STRIP : (q + 1) * STRIP]
        if b == 0:
            pl.semaphore_wait(barrier, 7 + 7 + NX - 1)
        for d in (2, 1, 3):
            copy = pltpu.make_async_remote_copy(
                src_ref=fsend.at[b, rem(x + d, NX)], dst_ref=xrecv.at[b, d - 1],
                send_sem=xs_sem.at[b, d - 1], recv_sem=xr_sem.at[b, d - 1],
                device_id=beside(d), device_id_type=MESH)
            copy.start()
            sends.append(copy)
        if b == 0:
            for dy, dc in around:
                pl.semaphore_signal(ready, inc=1, device_id=plane(dy, dc), device_id_type=MESH)

    pl.semaphore_wait(ready, 7)
    for b in range(CHUNKS):
        total = fsend[b, x].astype(F32)
        for d, at in ((1, 1), (3, 2), (2, 0)):
            sends[b * 3 + at].wait_recv()
            total = total + xrecv[b, d - 1].astype(F32)
        summed[b] = total.astype(BF16)

        @pl.loop(0, 4)
        def _(k):
            pair = rem(div(z, 2) + 2 + k, 4)
            to_z, to_core = pair * 2 + b % 2, b // 2
            for block in range(BLOCKS):
                src = summed.at[b, pl.ds(pl.multiple_of(pair * 16, 16), 16), pl.ds(block * 128, 128)]
                to_y = rem(pair + block, NY)
                mine = jnp.logical_and(jnp.logical_and(to_z == z, to_y == y), to_core == core)

                @pl.when(mine)
                def _():
                    pltpu.make_async_copy(src, mid.at[here], ur_sem).start()

                @pl.when(jnp.logical_not(mine))
                def _():
                    pltpu.make_async_remote_copy(
                        src_ref=src, dst_ref=mid.at[here], send_sem=us_sem, recv_sem=ur_sem,
                        device_id=device(to_z, x, to_y, to_core), device_id_type=MESH).start()

    @pl.when(my_block < BLOCKS)
    def _():
        pltpu.make_async_copy(mid, mid, ur_sem).wait()
        both = jnp.dot(out_tab[...], mid[...].reshape(1024, 128), preferred_element_type=F32)
        forward = (both[: 2 * NB] + both[2 * NB :]).astype(BF16)
        twice = jnp.concatenate([forward, forward], axis=0)
        gsend[...] = jnp.dot(back_tab[...], twice, preferred_element_type=F32).astype(BF16).reshape(ROWS, 16, 128)
        dst = gbuf.at[pl.ds(pl.multiple_of(my_chunk * CR + my_pair * 16, 16), 16),
                      pl.ds(pl.multiple_of(x * STRIP + my_block * 128, 128), 128)]
        pltpu.make_async_copy(gsend.at[row], dst, gr_sem.at[my_chunk]).start()

        @pl.loop(0, NZ)
        def _(k):
            to_z = rem(z + far8(k), NZ)

            def send(dy, dc):
                to_y, to_core = rem(y + dy, NY), core if dc == 0 else 1 - core
                to = device(to_z, x, to_y, to_core)
                pltpu.make_async_remote_copy(
                    src_ref=gsend.at[to[0]], dst_ref=dst, send_sem=gs_sem, recv_sem=gr_sem.at[my_chunk],
                    device_id=to, device_id_type=MESH).start()

            for dy, dc in around:
                send(dy, dc)

            @pl.when(k < NZ - 1)
            def _():
                send(0, 0)

    gathers, swaps = [], []
    for b in range(CHUNKS):
        block = gbuf.at[pl.ds(b * CR, CR), pl.ds(pl.multiple_of(x * STRIP, 128), STRIP)]
        pltpu.make_async_copy(block, block, gr_sem.at[b]).wait()
        for d in (2, 1, 3):
            copy = pltpu.make_async_remote_copy(
                src_ref=block, dst_ref=block, send_sem=as_sem.at[b, d - 1], recv_sem=ar_sem.at[b, d - 1],
                device_id=beside(d), device_id_type=MESH)
            copy.start()
            gathers.append(copy)
    fold = jnp.concatenate([expand, jnp.zeros((256 - TILE, TILE * OWN), BF16)], axis=0)
    own_k = (k_row == k_lane)[:CR]
    lines = jnp.broadcast_to(last[...][:, None, :], (NB // 2, PC, 2 * CR)).reshape(NB // 2 * PC, 2 * CR)
    p_row = lax.broadcasted_iota(jnp.int32, lines.shape, 0) % PC
    p_lane = (lax.broadcasted_iota(jnp.int32, lines.shape, 1) // KC) % PC
    lines = jnp.where(p_row == p_lane, lines, 0.0)
    high = lines.astype(BF16)
    lines = jnp.concatenate([high, (lines - high.astype(F32)).astype(BF16)], axis=1)
    chip = rem(z, 4) * 4 + y

    def swap_of(b):
        for copy in gathers[b * 3 : b * 3 + 3]:
            copy.wait_recv()
        got = lax.dot_general(gbuf[b * CR : (b + 1) * CR, :], flat[...], (((1,), (1,)), ((), ())),
                              preferred_element_type=F32)
        got = jnp.where(own_k, got, 0.0).astype(BF16)
        hx[b, core] = lax.dot_general(got, fold, (((1,), (1,)), ((), ())), preferred_element_type=F32).astype(BF16)
        swap = pltpu.make_async_remote_copy(
            src_ref=hx.at[b, core], dst_ref=hx.at[b, core], send_sem=hs_sem.at[b], recv_sem=hr_sem.at[b],
            device_id=device(z, x, y, 1 - core), device_id_type=MESH)
        swap.start()
        swaps.append(swap)

    def blocks_of(b):
        swaps[b].wait_recv()
        pair = hx[b].reshape(2 * CR, 256)
        got = jnp.dot(lines, jnp.concatenate([pair, pair], axis=0), preferred_element_type=F32)
        got = jnp.concatenate([got[:, :128].reshape(16, PC, 128), got[:, 128:].reshape(16, PC, 128)], axis=1)
        bsend[b] = got.astype(BF16)
        pltpu.make_async_copy(bsend.at[b, chip], brecv.at[b, chip], br_sem.at[b]).start()

        @pl.loop(0, 4)
        def _(k):
            low = rem(rem(z, 4) + 2 + k, 4)
            for dy in FAR4:
                to_y = rem(y + dy, NY)

                def send():
                    pltpu.make_async_remote_copy(
                        src_ref=bsend.at[b, low * 4 + to_y], dst_ref=brecv.at[b, chip],
                        send_sem=bs_sem.at[b], recv_sem=br_sem.at[b],
                        device_id=device(div(z, 4) * 4 + low, x, to_y, core), device_id_type=MESH).start()

                if dy:
                    send()
                else:
                    pl.when(k != 2)(send)

    for b in range(CHUNKS):
        swap_of(b)
        if b:
            blocks_of(b - 1)
    blocks_of(CHUNKS - 1)
    mine = []
    for b in range(CHUNKS):
        pltpu.make_async_copy(brecv.at[b], brecv.at[b], br_sem.at[b]).wait()
        got = jnp.sum(brecv[b].astype(F32), axis=0)
        mine.append(jnp.concatenate([got[:PC], got[PC:]], axis=1))
    mine = jnp.concatenate(mine, axis=0)

    group = lax.broadcasted_iota(jnp.int32, (8, 128), 1) // PS
    gram = lax.dot_general(mine, jnp.concatenate([mine] * 4, axis=0), (((1,), (1,)), ((), ())),
                           precision=HIGHEST, preferred_element_type=F32)
    packed = gram[0:8]
    for n in range(1, 4):
        packed = jnp.where(group == n, gram[n * 8 : n * 8 + 8], packed)

    def add_up(buf, stage):
        some = buf.at[pl.ds(0, 15)]
        pltpu.make_async_copy(some, some, qr_sem.at[stage]).wait()
        return jnp.sum(buf[...], axis=0)

    def share(buf, me, stage, to):
        pltpu.make_async_remote_copy(
            src_ref=buf.at[me], dst_ref=buf.at[me], send_sem=qs_sem.at[stage], recv_sem=qr_sem.at[stage],
            device_id=to, device_id_type=MESH).start()

    gz[z * 2 + core] = packed
    for d in FAR8:
        for dc in (1, 0):
            if d or dc:
                share(gz, z * 2 + core, 0, device(rem(z + d, NZ), x, y, core if dc == 0 else 1 - core))
    packed = add_up(gz, 0)
    gx[x * 4 + y] = packed
    for dx in FAR4:
        for dy in FAR4:
            if dx or dy:
                share(gx, x * 4 + y, 1, device(z, rem(x + dx, NX), rem(y + dy, NY), core))
    packed = add_up(gx, 1)

    turned = [packed] + [pltpu.roll(packed, n * PS, 1) for n in range(1, 4)]
    strips = []
    for n in range(4):
        strip = turned[(4 - n) % 4]
        for g in range(1, 4):
            strip = jnp.where(group == g, turned[(g - n) % 4], strip)
        strips.append(strip)
    gram = jnp.concatenate(strips, axis=0)
    s_row = lax.broadcasted_iota(jnp.int32, (PS, 128), 0)
    s_lane = lax.broadcasted_iota(jnp.int32, (PS, 128), 1)
    eye = jnp.where(s_row == s_lane % PS, 1.0, 0.0)
    scale = jnp.sum(jnp.where(s_row == s_lane, gram, 0.0), keepdims=True) + 1e-06

    def left(a):
        high = a.astype(BF16).astype(F32)
        lane = lax.broadcasted_iota(jnp.int32, a.shape, 1)
        return jnp.where(lane < 64, high, a - high).astype(BF16)

    def right(a):
        high = a.astype(BF16)
        low = (a - high.astype(F32)).astype(BF16)
        return jnp.concatenate([high, low, high, low], axis=0)

    square = gram / scale
    inverse = eye
    for step in range(NSTEPS):
        weight = 1.5 * eye - 0.5 * square
        factor = right(weight)
        both = jnp.dot(left(jnp.concatenate([square, inverse], axis=0)), factor, preferred_element_type=F32)
        inverse = both[PS:]
        if step < NSTEPS - 1:
            square = jnp.dot(left(both[:PS]), factor, preferred_element_type=F32)
    answer = jnp.dot(left(inverse), right(mine), preferred_element_type=F32)
    result[...] = answer[:, :TILE] * (math.sqrt(NB * M) / jnp.sqrt(scale))

    for copy in sends + gathers + swaps:
        copy.wait_send()
    for stage, buf in enumerate((gz, gx)):
        some = buf.at[pl.ds(0, 15)]
        pltpu.make_async_copy(some, some, qs_sem.at[stage]).wait()
    for b in range(CHUNKS):
        rest = bsend.at[b, pl.ds(0, 15)]
        pltpu.make_async_copy(rest, rest, bs_sem.at[b]).wait()

    @pl.when(my_block < BLOCKS)
    def _():
        most = mid.at[pl.ds(0, 47)]
        pltpu.make_async_copy(most, most, us_sem).wait()
        most = mid.at[pl.ds(0, 63)]
        pltpu.make_async_copy(most, most, gs_sem).wait()

    @pl.when(my_block >= BLOCKS)
    def _():
        most = mid.at[pl.ds(0, 48)]
        pltpu.make_async_copy(most, most, us_sem).wait()


def shards(damping, block_seeds):
    mix, out, back, last = tables()
    vmem, anywhere = pl.BlockSpec(memory_space=pltpu.VMEM), pl.BlockSpec(memory_space=pl.ANY)
    dma = pltpu.SemaphoreType.DMA
    turned = pl.pallas_call(
        kernel,
        out_shape=jax.ShapeDtypeStruct((PS, TILE), F32),
        in_specs=[pl.BlockSpec(memory_space=pltpu.SMEM)] + [anywhere] * 5,
        out_specs=vmem,
        scratch_shapes=[
            pltpu.VMEM((TILE, OWN, M), BF16),
            pltpu.VMEM((TILE * OWN, M), BF16),
            pltpu.VMEM((KC, NB * PS), F32),
            pltpu.VMEM((16, 2 * CR), F32),
            pltpu.VMEM((4 * NB, 1024), BF16),
            pltpu.VMEM((512, 4 * NB), BF16),
            pltpu.VMEM((NB * PS, TILE), BF16),
            pltpu.VMEM((CHUNKS, NX, CR, STRIP), BF16),
            pltpu.VMEM((CHUNKS, NX - 1, CR, STRIP), BF16),
            pltpu.VMEM((CHUNKS, CR, STRIP), BF16),
            pltpu.VMEM((64, 16, 128), BF16),
            pltpu.VMEM((ROWS, 16, 128), BF16),
            pltpu.VMEM((PS * KC, M), BF16),
            pltpu.VMEM((CHUNKS, 2, CR, 256), BF16),
            pltpu.VMEM((CHUNKS, 16, 16, 128), BF16),
            pltpu.VMEM((CHUNKS, 16, 16, 128), BF16),
            pltpu.VMEM((16, 8, 128), F32),
            pltpu.VMEM((16, 8, 128), F32),
            pltpu.SemaphoreType.REGULAR, dma((5,)), dma((CHUNKS, 3)), dma((CHUNKS, 3)), dma, dma, dma,
            dma((CHUNKS,)), dma((CHUNKS, 3)), dma((CHUNKS, 3)), dma((CHUNKS,)), dma((CHUNKS,)),
            dma((CHUNKS,)), dma((CHUNKS,)), dma((2,)), dma((2,)),
        ],
        compiler_params=pltpu.CompilerParams(
            collective_id=0, has_side_effects=True, vmem_limit_bytes=62 << 20),
        name="hankel",
    )(block_seeds, damping, jnp.asarray(mix), jnp.asarray(out), jnp.asarray(back), jnp.asarray(last))
    return turned.T[None]


def solution(mesh):
    return jax.shard_map(
        shards,
        mesh=mesh,
        in_specs=(P("col", "row", None), P()),
        out_specs=P("row", "col", None),
        check_vma=False,
    )
```

```python
import functools
import math

import jax
import jax.numpy as jnp
import numpy as np
from jax import lax
from jax.experimental import pallas as pl
from jax.experimental.pallas import tpu as pltpu
from jax.sharding import PartitionSpec as P

NF = 128
M = 1536
PS = 32
NB = 32
NSTEPS = 12
PRIME = 65521
OWN = 4
KC = 2 * OWN
ROWS = 32
TILE = 192
NX, NY, NZ = 4, 4, 8
CHUNKS = 4
PC = PS // CHUNKS
CR = PC * KC
BLOCKS = 3
STRIP = BLOCKS * 128
MESH = pl.DeviceIdType.MESH
F32, BF16 = jnp.float32, jnp.bfloat16
HIGHEST = lax.Precision.HIGHEST


def wave(step, sign):
    freq = np.arange(NF)[:, None] + 0.5
    angle = math.pi * freq * step[None, :] / NF
    window = np.exp(-math.log(3.0) * step / NB)[None, :]
    return np.stack([np.cos(angle) * window, sign * np.sin(angle) * window], 1).reshape(2 * NF, len(step))


def halves(table):
    high = table.astype(jnp.bfloat16)
    low = (table - high.astype(np.float64)).astype(jnp.bfloat16)
    return high, low


def tables():
    step = np.arange(NB).astype(np.float64)
    amp = math.sqrt(2.0 / NF) / math.sqrt(NB * M)
    mix = np.repeat(wave(step, 1.0), PS, axis=1).astype(np.float32)
    same = np.eye(2)
    out = (amp * wave(step, -1.0)).reshape(ROWS, KC, NB)
    out = np.einsum("akj,pq->pjaqk", out, same).reshape(2 * NB, ROWS * 2 * KC)
    out = np.concatenate([out, out], axis=1)
    out = np.concatenate(halves(out), axis=0)
    back = (amp * wave(step + 1.0, 1.0)).reshape(ROWS, KC, NB)
    back = np.einsum("akj,pq->apkqj", back, same).reshape(ROWS * 2 * KC, 2 * NB)
    back = np.concatenate(halves(back), axis=1)
    last = wave(step, -1.0).reshape(ROWS // 2, 2, KC, NB // 2, 2)
    last = last.transpose(0, 4, 3, 1, 2)
    last = np.broadcast_to(last[:, :, :, :, None, :], last.shape[:4] + (PC, KC))
    last = last.reshape(ROWS * (NB // 2), 2 * CR).astype(np.float32)
    return mix, out, back, last


def sine_terms():
    t = np.cos(np.pi * (np.arange(400) + 0.5) / 400) * 0.5
    t = t[t > 0]
    u = t * t
    basis = np.stack([u**n for n in range(5)], 1)
    return [float(v) for v in np.linalg.lstsq(basis, np.sin(np.pi * t) / t, rcond=None)[0]]


SINE = sine_terms()


def residue(x):
    q = (x.astype(F32) * (1.0 / PRIME)).astype(jnp.int32)
    r = x - q * PRIME
    r = jnp.where(r < 0, r + PRIME, r)
    return jnp.where(r >= PRIME, r - PRIME, r)


FAR4 = (2, 1, 3, 0)
FAR8 = (4, 3, 5, 2, 6, 1, 7, 0)


def rem(a, n):
    return lax.rem(a, jnp.int32(n))


def div(a, n):
    return lax.div(a, jnp.int32(n))


def far8(k):
    half = div(k + 1, 2)
    return 4 + half - 2 * half * rem(k, 2)


def place():
    r, c = lax.axis_index("row"), lax.axis_index("col")
    return div(c, 4) * 4 + div(r, 8), rem(c, 4), rem(div(r, 2), 4), rem(r, 2)


def device(z, x, y, core):
    return (rem(z, 4) * 8 + y * 2 + core, div(z, 4) * 4 + x)


def kernel(seeds_hbm, damp_hbm, mix_hbm, out_hbm, back_hbm, last_hbm, result,
           seeds, damp, flat, mix, last, out_tab, back_tab, probes, fsend, xrecv, summed, mid, gsend, gbuf,
           hx, bsend, brecv, gz, gx,
           ready, load_sem, xs_sem, xr_sem, us_sem, ur_sem, gs_sem, gr_sem, as_sem, ar_sem,
           hs_sem, hr_sem, bs_sem, br_sem, qs_sem, qr_sem):
    z, x, y, core = place()
    row, col = lax.axis_index("row"), lax.axis_index("col")
    here = z * 8 + y * 2 + core
    my_chunk, my_pair, my_block = core * 2 + rem(z, 2), div(z, 2), rem(y + 4 - div(z, 2), NY)

    def beside(d):
        return device(z, rem(x + d, NX), y, core)

    def plane(dy, dc):
        return device(z, x, rem(y + dy, NY), core if dc == 0 else 1 - core)

    around = [(dy, dc) for dy in FAR4 for dc in (1, 0) if dy or dc]

    loads = [
        pltpu.make_async_copy(damp_hbm, damp, load_sem.at[1]),
        pltpu.make_async_copy(mix_hbm.at[pl.ds(pl.multiple_of(row * KC, KC), KC)], mix, load_sem.at[0]),
        pltpu.make_async_copy(last_hbm.at[pl.ds(pl.multiple_of(row * 16, 16), 16)], last, load_sem.at[2]),
        pltpu.make_async_copy(out_hbm, out_tab, load_sem.at[3]),
        pltpu.make_async_copy(back_hbm, back_tab, load_sem.at[4]),
    ]
    seeding = pltpu.make_async_copy(seeds_hbm, seeds, load_sem.at[5])
    seeding.start()
    loads[0].start()
    barrier = pltpu.get_barrier_semaphore()
    for d in FAR8[:-1]:
        pl.semaphore_signal(barrier, inc=1, device_id=device(rem(z + d, NZ), x, y, core), device_id_type=MESH)
    for dy, dc in around:
        pl.semaphore_signal(barrier, inc=1, device_id=plane(dy, dc), device_id_type=MESH)
    for d in FAR4[:-1]:
        pl.semaphore_signal(barrier, inc=1, device_id=beside(d), device_id_type=MESH)
    for load in loads[1:]:
        load.start()
    seeding.wait()

    column = col * TILE + lax.broadcasted_iota(jnp.int32, (1, TILE), 1)
    pcol = lax.broadcasted_iota(jnp.int32, (PS, 1), 0)
    pone = (pcol + 1).astype(F32)

    @pl.loop(0, NB)
    def _(j):
        s = seeds[j]
        inner = residue(residue(s * (column + 1)) * (column + 3)).astype(F32)
        second = (residue(s * (pcol + 1)) * (pcol + 2)).astype(F32)
        phase = inner * pone + second
        phase = phase - jnp.floor(phase * (1.0 / PRIME) + 0.5) * PRIME
        t = phase * (1.0 / PRIME)
        u = t * t
        poly = SINE[4]
        for n in (3, 2, 1, 0):
            poly = poly * u + SINE[n]
        sine = poly * t
        probes[pl.ds(pl.multiple_of(j * PS, PS), PS), :] = (1.0 - 2.0 * sine * sine).astype(BF16)

    loads[1].wait()
    spread = jnp.broadcast_to(mix[...][None], (PS, KC, NB * PS)).reshape(PS * KC, NB * PS)
    r_idx = lax.broadcasted_iota(jnp.int32, (PS * KC, NB * PS), 0) // KC
    l_idx = lax.broadcasted_iota(jnp.int32, (PS * KC, NB * PS), 1) % PS
    spread = jnp.where(r_idx == l_idx, spread, 0.0).astype(BF16)
    terms = jnp.dot(spread, probes[...], preferred_element_type=F32).astype(BF16)
    wide = lax.broadcasted_iota(jnp.int32, (TILE, TILE * OWN), 1) // OWN
    tall = lax.broadcasted_iota(jnp.int32, (TILE, TILE * OWN), 0)
    expand = jnp.where(wide == tall, 1.0, 0.0).astype(BF16)
    k_row = (lax.broadcasted_iota(jnp.int32, (PS * KC, TILE * OWN), 0) % KC) // 2
    k_lane = lax.broadcasted_iota(jnp.int32, (PS * KC, TILE * OWN), 1) % OWN
    terms = jnp.dot(terms, expand, preferred_element_type=F32)
    terms = jnp.where(k_row == k_lane, terms, 0.0).astype(BF16)

    loads[0].wait()
    for n in range(3):
        flat[:, n * 512 : (n + 1) * 512] = damp[:, :, n * 512 : (n + 1) * 512].reshape(TILE * OWN, 512)
    for load in loads[2:]:
        load.wait()
    sends = []
    for b in range(CHUNKS):
        for d in FAR4:
            q = rem(x + d, NX)
            part = flat[:, pl.ds(pl.multiple_of(q * STRIP, 128), STRIP)]
            got = jnp.dot(terms[b * CR : (b + 1) * CR], part, preferred_element_type=F32)
            fsend[b, q] = got.astype(BF16)
            if d == 0:
                continue
            if b == 0 and d == FAR4[0]:
                pl.semaphore_wait(barrier, 7 + 7 + NX - 1)
            copy = pltpu.make_async_remote_copy(
                src_ref=fsend.at[b, q], dst_ref=xrecv.at[b, d - 1],
                send_sem=xs_sem.at[b, d - 1], recv_sem=xr_sem.at[b, d - 1],
                device_id=beside(d), device_id_type=MESH)
            copy.start()
            sends.append(copy)
        if b == 0:
            for dy, dc in around:
                pl.semaphore_signal(ready, inc=1, device_id=plane(dy, dc), device_id_type=MESH)

    pl.semaphore_wait(ready, 7)
    for b in range(CHUNKS):
        total = fsend[b, x].astype(F32)
        for d, at in ((1, 1), (3, 2), (2, 0)):
            sends[b * 3 + at].wait_recv()
            total = total + xrecv[b, d - 1].astype(F32)
        summed[b] = total.astype(BF16)

        @pl.loop(0, 4)
        def _(k):
            pair = rem(div(z, 2) + 2 + k, 4)
            to_z, to_core = pair * 2 + b % 2, b // 2
            for block in range(BLOCKS):
                src = summed.at[b, pl.ds(pl.multiple_of(pair * 16, 16), 16), pl.ds(block * 128, 128)]
                to_y = rem(pair + block, NY)
                mine = jnp.logical_and(jnp.logical_and(to_z == z, to_y == y), to_core == core)

                @pl.when(mine)
                def _():
                    pltpu.make_async_copy(src, mid.at[here], ur_sem).start()

                @pl.when(jnp.logical_not(mine))
                def _():
                    pltpu.make_async_remote_copy(
                        src_ref=src, dst_ref=mid.at[here], send_sem=us_sem, recv_sem=ur_sem,
                        device_id=device(to_z, x, to_y, to_core), device_id_type=MESH).start()

    @pl.when(my_block < BLOCKS)
    def _():
        pltpu.make_async_copy(mid, mid, ur_sem).wait()
        both = jnp.dot(out_tab[...], mid[...].reshape(1024, 128), preferred_element_type=F32)
        forward = (both[: 2 * NB] + both[2 * NB :]).astype(BF16)
        twice = jnp.concatenate([forward, forward], axis=0)
        gsend[...] = jnp.dot(back_tab[...], twice, preferred_element_type=F32).astype(BF16).reshape(ROWS, 16, 128)
        dst = gbuf.at[pl.ds(pl.multiple_of(my_chunk * CR + my_pair * 16, 16), 16),
                      pl.ds(pl.multiple_of(x * STRIP + my_block * 128, 128), 128)]
        pltpu.make_async_copy(gsend.at[row], dst, gr_sem.at[my_chunk]).start()

        @pl.loop(0, NZ)
        def _(k):
            to_z = rem(z + far8(k), NZ)

            def send(dy, dc):
                to_y, to_core = rem(y + dy, NY), core if dc == 0 else 1 - core
                to = device(to_z, x, to_y, to_core)
                pltpu.make_async_remote_copy(
                    src_ref=gsend.at[to[0]], dst_ref=dst, send_sem=gs_sem, recv_sem=gr_sem.at[my_chunk],
                    device_id=to, device_id_type=MESH).start()

            for dy, dc in around:
                send(dy, dc)

            @pl.when(k < NZ - 1)
            def _():
                send(0, 0)

    gathers, swaps = [], []
    for b in range(CHUNKS):
        block = gbuf.at[pl.ds(b * CR, CR), pl.ds(pl.multiple_of(x * STRIP, 128), STRIP)]
        pltpu.make_async_copy(block, block, gr_sem.at[b]).wait()
        for d in (2, 1, 3):
            copy = pltpu.make_async_remote_copy(
                src_ref=block, dst_ref=block, send_sem=as_sem.at[b, d - 1], recv_sem=ar_sem.at[b, d - 1],
                device_id=beside(d), device_id_type=MESH)
            copy.start()
            gathers.append(copy)
    fold = jnp.concatenate([expand, jnp.zeros((256 - TILE, TILE * OWN), BF16)], axis=0)
    own_k = (k_row == k_lane)[:CR]
    lines = jnp.broadcast_to(last[...][:, None, :], (NB // 2, PC, 2 * CR)).reshape(NB // 2 * PC, 2 * CR)
    p_row = lax.broadcasted_iota(jnp.int32, lines.shape, 0) % PC
    p_lane = (lax.broadcasted_iota(jnp.int32, lines.shape, 1) // KC) % PC
    lines = jnp.where(p_row == p_lane, lines, 0.0)
    high = lines.astype(BF16)
    lines = jnp.concatenate([high, (lines - high.astype(F32)).astype(BF16)], axis=1)
    chip = rem(z, 4) * 4 + y

    def swap_of(b):
        got = jnp.zeros((CR, TILE * OWN), F32)
        for d, at in ((0, None), (1, 1), (3, 2), (2, 0)):
            if d:
                gathers[b * 3 + at].wait_recv()
            strip = pl.ds(pl.multiple_of(rem(x + NX - d, NX) * STRIP, 128), STRIP)
            got = got + lax.dot_general(gbuf[b * CR : (b + 1) * CR, strip], flat[:, strip],
                                        (((1,), (1,)), ((), ())), preferred_element_type=F32)
        got = jnp.where(own_k, got, 0.0).astype(BF16)
        hx[b, core] = lax.dot_general(got, fold, (((1,), (1,)), ((), ())), preferred_element_type=F32).astype(BF16)
        swap = pltpu.make_async_remote_copy(
            src_ref=hx.at[b, core], dst_ref=hx.at[b, core], send_sem=hs_sem.at[b], recv_sem=hr_sem.at[b],
            device_id=device(z, x, y, 1 - core), device_id_type=MESH)
        swap.start()
        swaps.append(swap)

    def blocks_of(b):
        swaps[b].wait_recv()
        pair = hx[b].reshape(2 * CR, 256)
        got = jnp.dot(lines, jnp.concatenate([pair, pair], axis=0), preferred_element_type=F32)
        got = jnp.concatenate([got[:, :128].reshape(16, PC, 128), got[:, 128:].reshape(16, PC, 128)], axis=1)
        bsend[b] = got.astype(BF16)
        pltpu.make_async_copy(bsend.at[b, chip], brecv.at[b, chip], br_sem.at[b]).start()

        @pl.loop(0, 4)
        def _(k):
            low = rem(rem(z, 4) + 2 + k, 4)
            for dy in FAR4:
                to_y = rem(y + dy, NY)

                def send():
                    pltpu.make_async_remote_copy(
                        src_ref=bsend.at[b, low * 4 + to_y], dst_ref=brecv.at[b, chip],
                        send_sem=bs_sem.at[b], recv_sem=br_sem.at[b],
                        device_id=device(div(z, 4) * 4 + low, x, to_y, core), device_id_type=MESH).start()

                if dy:
                    send()
                else:
                    pl.when(k != 2)(send)

    for b in range(CHUNKS):
        swap_of(b)
        if b:
            blocks_of(b - 1)
    blocks_of(CHUNKS - 1)
    mine = []
    for b in range(CHUNKS):
        pltpu.make_async_copy(brecv.at[b], brecv.at[b], br_sem.at[b]).wait()
        got = jnp.sum(brecv[b].astype(F32), axis=0)
        mine.append(jnp.concatenate([got[:PC], got[PC:]], axis=1))
    mine = jnp.concatenate(mine, axis=0)

    group = lax.broadcasted_iota(jnp.int32, (8, 128), 1) // PS
    gram = lax.dot_general(mine, jnp.concatenate([mine] * 4, axis=0), (((1,), (1,)), ((), ())),
                           precision=HIGHEST, preferred_element_type=F32)
    packed = gram[0:8]
    for n in range(1, 4):
        packed = jnp.where(group == n, gram[n * 8 : n * 8 + 8], packed)

    def add_up(buf, stage):
        some = buf.at[pl.ds(0, 15)]
        pltpu.make_async_copy(some, some, qr_sem.at[stage]).wait()
        return jnp.sum(buf[...], axis=0)

    def share(buf, me, stage, to):
        pltpu.make_async_remote_copy(
            src_ref=buf.at[me], dst_ref=buf.at[me], send_sem=qs_sem.at[stage], recv_sem=qr_sem.at[stage],
            device_id=to, device_id_type=MESH).start()

    gz[z * 2 + core] = packed
    for d in FAR8:
        for dc in (1, 0):
            if d or dc:
                share(gz, z * 2 + core, 0, device(rem(z + d, NZ), x, y, core if dc == 0 else 1 - core))
    for copy in sends + gathers + swaps:
        copy.wait_send()

    @pl.when(my_block < BLOCKS)
    def _():
        most = mid.at[pl.ds(0, 47)]
        pltpu.make_async_copy(most, most, us_sem).wait()
        most = mid.at[pl.ds(0, 63)]
        pltpu.make_async_copy(most, most, gs_sem).wait()

    @pl.when(my_block >= BLOCKS)
    def _():
        most = mid.at[pl.ds(0, 48)]
        pltpu.make_async_copy(most, most, us_sem).wait()

    packed = add_up(gz, 0)
    gx[x * 4 + y] = packed
    for dx in FAR4:
        for dy in FAR4:
            if dx or dy:
                share(gx, x * 4 + y, 1, device(z, rem(x + dx, NX), rem(y + dy, NY), core))
    for b in range(CHUNKS):
        rest = bsend.at[b, pl.ds(0, 15)]
        pltpu.make_async_copy(rest, rest, bs_sem.at[b]).wait()
    packed = add_up(gx, 1)
    for stage, buf in enumerate((gz, gx)):
        some = buf.at[pl.ds(0, 15)]
        pltpu.make_async_copy(some, some, qs_sem.at[stage]).wait()

    turned = [packed] + [pltpu.roll(packed, n * PS, 1) for n in range(1, 4)]
    strips = []
    for n in range(4):
        strip = turned[(4 - n) % 4]
        for g in range(1, 4):
            strip = jnp.where(group == g, turned[(g - n) % 4], strip)
        strips.append(strip)
    gram = jnp.concatenate(strips, axis=0)
    s_row = lax.broadcasted_iota(jnp.int32, (PS, 128), 0)
    s_lane = lax.broadcasted_iota(jnp.int32, (PS, 128), 1)
    eye = jnp.where(s_row == s_lane % PS, 1.0, 0.0)
    scale = jnp.sum(jnp.where(s_row == s_lane, gram, 0.0), keepdims=True) + 1e-06

    def left(a):
        high = a.astype(BF16).astype(F32)
        lane = lax.broadcasted_iota(jnp.int32, a.shape, 1)
        return jnp.where(lane < 64, high, a - high).astype(BF16)

    def right(a):
        high = a.astype(BF16)
        low = (a - high.astype(F32)).astype(BF16)
        return jnp.concatenate([high, low, high, low], axis=0)

    square = gram / scale
    inverse = eye
    for step in range(NSTEPS):
        weight = 1.5 * eye - 0.5 * square
        factor = right(weight)
        both = jnp.dot(left(jnp.concatenate([square, inverse], axis=0)), factor, preferred_element_type=F32)
        inverse = both[PS:]
        if step < NSTEPS - 1:
            square = jnp.dot(left(both[:PS]), factor, preferred_element_type=F32)
    answer = jnp.dot(left(inverse), right(mine), preferred_element_type=F32)
    result[...] = answer[:, :TILE] * (math.sqrt(NB * M) / jnp.sqrt(scale))


def shards(damping, block_seeds):
    mix, out, back, last = tables()
    vmem, hbm = pl.BlockSpec(memory_space=pltpu.VMEM), pl.BlockSpec(memory_space=pltpu.HBM)
    dma = pltpu.SemaphoreType.DMA
    turned = pl.pallas_call(
        kernel,
        out_shape=jax.ShapeDtypeStruct((PS, TILE), F32),
        in_specs=[hbm] * 6,
        out_specs=vmem,
        scratch_shapes=[
            pltpu.SMEM((NB,), jnp.int32),
            pltpu.VMEM((TILE, OWN, M), BF16),
            pltpu.VMEM((TILE * OWN, M), BF16),
            pltpu.VMEM((KC, NB * PS), F32),
            pltpu.VMEM((16, 2 * CR), F32),
            pltpu.VMEM((4 * NB, 1024), BF16),
            pltpu.VMEM((512, 4 * NB), BF16),
            pltpu.VMEM((NB * PS, TILE), BF16),
            pltpu.VMEM((CHUNKS, NX, CR, STRIP), BF16),
            pltpu.VMEM((CHUNKS, NX - 1, CR, STRIP), BF16),
            pltpu.VMEM((CHUNKS, CR, STRIP), BF16),
            pltpu.VMEM((64, 16, 128), BF16),
            pltpu.VMEM((ROWS, 16, 128), BF16),
            pltpu.VMEM((PS * KC, M), BF16),
            pltpu.VMEM((CHUNKS, 2, CR, 256), BF16),
            pltpu.VMEM((CHUNKS, 16, 16, 128), BF16),
            pltpu.VMEM((CHUNKS, 16, 16, 128), BF16),
            pltpu.VMEM((16, 8, 128), F32),
            pltpu.VMEM((16, 8, 128), F32),
            pltpu.SemaphoreType.REGULAR, dma((6,)), dma((CHUNKS, 3)), dma((CHUNKS, 3)), dma, dma, dma,
            dma((CHUNKS,)), dma((CHUNKS, 3)), dma((CHUNKS, 3)), dma((CHUNKS,)), dma((CHUNKS,)),
            dma((CHUNKS,)), dma((CHUNKS,)), dma((2,)), dma((2,)),
        ],
        compiler_params=pltpu.CompilerParams(
            collective_id=0, has_side_effects=True, vmem_limit_bytes=40 << 20),
        name="hankel",
    )(block_seeds, damping, jnp.asarray(mix), jnp.asarray(out), jnp.asarray(back), jnp.asarray(last))
    return turned.T[None]


def solution(mesh):
    return jax.shard_map(
        shards,
        mesh=mesh,
        in_specs=(P("col", "row", None), P()),
        out_specs=P("row", "col", None),
        check_vma=False,
    )
```

```python
import functools
import math

import jax
import jax.numpy as jnp
import numpy as np
from jax import lax
from jax.experimental import pallas as pl
from jax.experimental.pallas import tpu as pltpu
from jax.sharding import PartitionSpec as P

NF = 128
M = 1536
PS = 32
NB = 32
NSTEPS = 12
PRIME = 65521
OWN = 4
KC = 2 * OWN
ROWS = 32
TILE = 192
NX, NY, NZ = 4, 4, 8
CHUNKS = 4
PC = PS // CHUNKS
CR = PC * KC
BLOCKS = 3
STRIP = BLOCKS * 128
MESH = pl.DeviceIdType.MESH
F32, BF16 = jnp.float32, jnp.bfloat16
HIGHEST = lax.Precision.HIGHEST


def wave(step, sign):
    freq = np.arange(NF)[:, None] + 0.5
    angle = math.pi * freq * step[None, :] / NF
    window = np.exp(-math.log(3.0) * step / NB)[None, :]
    return np.stack([np.cos(angle) * window, sign * np.sin(angle) * window], 1).reshape(2 * NF, len(step))


def halves(table):
    high = table.astype(jnp.bfloat16)
    low = (table - high.astype(np.float64)).astype(jnp.bfloat16)
    return high, low


def tables():
    step = np.arange(NB).astype(np.float64)
    amp = math.sqrt(2.0 / NF) / math.sqrt(NB * M)
    mix = np.repeat(wave(step, 1.0), PS, axis=1).astype(np.float32)
    same = np.eye(2)
    out = (amp * wave(step, -1.0)).reshape(ROWS, KC, NB)
    out = np.einsum("akj,pq->pjaqk", out, same).reshape(2 * NB, ROWS * 2 * KC)
    out = np.concatenate([out, out], axis=1)
    out = np.concatenate(halves(out), axis=0)
    back = (amp * wave(step + 1.0, 1.0)).reshape(ROWS, KC, NB)
    back = np.einsum("akj,pq->apkqj", back, same).reshape(ROWS * 2 * KC, 2 * NB)
    back = np.concatenate(halves(back), axis=1)
    last = wave(step, -1.0).reshape(ROWS // 2, 2, KC, NB // 2, 2)
    last = last.transpose(0, 4, 3, 1, 2)
    last = np.broadcast_to(last[:, :, :, :, None, :], last.shape[:4] + (PC, KC))
    last = last.reshape(ROWS * (NB // 2), 2 * CR).astype(np.float32)
    return mix, out, back, last


def sine_terms():
    t = np.cos(np.pi * (np.arange(400) + 0.5) / 400) * 0.5
    t = t[t > 0]
    u = t * t
    basis = np.stack([u**n for n in range(5)], 1)
    return [float(v) for v in np.linalg.lstsq(basis, np.sin(np.pi * t) / t, rcond=None)[0]]


SINE = sine_terms()


def residue(x):
    q = (x.astype(F32) * (1.0 / PRIME)).astype(jnp.int32)
    r = x - q * PRIME
    r = jnp.where(r < 0, r + PRIME, r)
    return jnp.where(r >= PRIME, r - PRIME, r)


FAR4 = (2, 1, 3, 0)
FAR8 = (4, 3, 5, 2, 6, 1, 7, 0)


def rem(a, n):
    return lax.rem(a, jnp.int32(n))


def div(a, n):
    return lax.div(a, jnp.int32(n))


def far8(k):
    half = div(k + 1, 2)
    return 4 + half - 2 * half * rem(k, 2)


def place():
    r, c = lax.axis_index("row"), lax.axis_index("col")
    return div(c, 4) * 4 + div(r, 8), rem(c, 4), rem(div(r, 2), 4), rem(r, 2)


def device(z, x, y, core):
    return (rem(z, 4) * 8 + y * 2 + core, div(z, 4) * 4 + x)


def kernel(facts, damp_hbm, mix_hbm, out_hbm, back_hbm, last_hbm, result,
           damp, flat, mix, last, out_tab, back_tab, probes, fsend, xrecv, summed, mid, gsend, gbuf,
           hx, bsend, brecv, gz, gx,
           ready, load_sem, xs_sem, xr_sem, us_sem, ur_sem, gs_sem, gr_sem, as_sem, ar_sem,
           hs_sem, hr_sem, bs_sem, br_sem, qs_sem, qr_sem):
    z, x, y, core = place()
    row = lax.axis_index("row")
    here = z * 8 + y * 2 + core
    my_chunk, my_pair, my_block = core * 2 + rem(z, 2), div(z, 2), rem(y + 4 - div(z, 2), NY)

    def beside(d):
        return device(z, rem(x + d, NX), y, core)

    def plane(dy, dc):
        return device(z, x, rem(y + dy, NY), core if dc == 0 else 1 - core)

    around = [(dy, dc) for dy in FAR4 for dc in (1, 0) if dy or dc]

    loads = [
        pltpu.make_async_copy(damp_hbm, damp, load_sem.at[1]),
        pltpu.make_async_copy(mix_hbm.at[pl.ds(pl.multiple_of(row * KC, KC), KC)], mix, load_sem.at[0]),
        pltpu.make_async_copy(last_hbm.at[pl.ds(pl.multiple_of(row * 16, 16), 16)], last, load_sem.at[2]),
        pltpu.make_async_copy(out_hbm, out_tab, load_sem.at[3]),
        pltpu.make_async_copy(back_hbm, back_tab, load_sem.at[4]),
    ]
    barrier = pltpu.get_barrier_semaphore()
    for d in FAR8[:-1]:
        pl.semaphore_signal(barrier, inc=1, device_id=device(rem(z + d, NZ), x, y, core), device_id_type=MESH)
    for dy, dc in around:
        pl.semaphore_signal(barrier, inc=1, device_id=plane(dy, dc), device_id_type=MESH)
    for d in FAR4[:-1]:
        pl.semaphore_signal(barrier, inc=1, device_id=beside(d), device_id_type=MESH)
    for load in loads:
        load.start()

    pone = (lax.broadcasted_iota(jnp.int32, (PS, 1), 0) + 1).astype(F32)
    second = jnp.transpose(facts[:, 128:])[TILE - 128 : TILE - 128 + PS]
    for j in range(NB):
        phase = facts[j : j + 1, :TILE] * pone + second[:, j : j + 1]
        phase = phase - jnp.floor(phase * (1.0 / PRIME) + 0.5) * PRIME
        t = phase * (1.0 / PRIME)
        u = t * t
        poly = SINE[4]
        for n in (3, 2, 1, 0):
            poly = poly * u + SINE[n]
        sine = poly * t
        probes[j * PS : (j + 1) * PS, :] = (1.0 - 2.0 * sine * sine).astype(BF16)

    loads[1].wait()
    spread = jnp.broadcast_to(mix[...][None], (PS, KC, NB * PS)).reshape(PS * KC, NB * PS)
    r_idx = lax.broadcasted_iota(jnp.int32, (PS * KC, NB * PS), 0) // KC
    l_idx = lax.broadcasted_iota(jnp.int32, (PS * KC, NB * PS), 1) % PS
    spread = jnp.where(r_idx == l_idx, spread, 0.0).astype(BF16)
    terms = jnp.dot(spread, probes[...], preferred_element_type=F32).astype(BF16)
    wide = lax.broadcasted_iota(jnp.int32, (TILE, TILE * OWN), 1) // OWN
    tall = lax.broadcasted_iota(jnp.int32, (TILE, TILE * OWN), 0)
    expand = jnp.where(wide == tall, 1.0, 0.0).astype(BF16)
    k_row = (lax.broadcasted_iota(jnp.int32, (PS * KC, TILE * OWN), 0) % KC) // 2
    k_lane = lax.broadcasted_iota(jnp.int32, (PS * KC, TILE * OWN), 1) % OWN
    terms = jnp.dot(terms, expand, preferred_element_type=F32)
    terms = jnp.where(k_row == k_lane, terms, 0.0).astype(BF16)

    loads[0].wait()
    for n in range(3):
        flat[:, n * 512 : (n + 1) * 512] = damp[:, :, n * 512 : (n + 1) * 512].reshape(TILE * OWN, 512)
    for load in loads[2:]:
        load.wait()
    sends = []
    for b in range(CHUNKS):
        got = jnp.dot(terms[b * CR : (b + 1) * CR], flat[...], preferred_element_type=F32).astype(BF16)
        for q in range(NX):
            fsend[b, q] = got[:, q * STRIP : (q + 1) * STRIP]
        if b == 0:
            pl.semaphore_wait(barrier, 7 + 7 + NX - 1)
        for d in (2, 1, 3):
            copy = pltpu.make_async_remote_copy(
                src_ref=fsend.at[b, rem(x + d, NX)], dst_ref=xrecv.at[b, d - 1],
                send_sem=xs_sem.at[b, d - 1], recv_sem=xr_sem.at[b, d - 1],
                device_id=beside(d), device_id_type=MESH)
            copy.start()
            sends.append(copy)
        if b == 0:
            for dy, dc in around:
                pl.semaphore_signal(ready, inc=1, device_id=plane(dy, dc), device_id_type=MESH)

    pl.semaphore_wait(ready, 7)
    for b in range(CHUNKS):
        total = fsend[b, x].astype(F32)
        for d, at in ((1, 1), (3, 2), (2, 0)):
            sends[b * 3 + at].wait_recv()
            total = total + xrecv[b, d - 1].astype(F32)
        summed[b] = total.astype(BF16)

        @pl.loop(0, 4)
        def _(k):
            pair = rem(div(z, 2) + 2 + k, 4)
            to_z, to_core = pair * 2 + b % 2, b // 2
            for block in range(BLOCKS):
                src = summed.at[b, pl.ds(pl.multiple_of(pair * 16, 16), 16), pl.ds(block * 128, 128)]
                to_y = rem(pair + block, NY)
                mine = jnp.logical_and(jnp.logical_and(to_z == z, to_y == y), to_core == core)

                @pl.when(mine)
                def _():
                    pltpu.make_async_copy(src, mid.at[here], ur_sem).start()

                @pl.when(jnp.logical_not(mine))
                def _():
                    pltpu.make_async_remote_copy(
                        src_ref=src, dst_ref=mid.at[here], send_sem=us_sem, recv_sem=ur_sem,
                        device_id=device(to_z, x, to_y, to_core), device_id_type=MESH).start()

    @pl.when(my_block < BLOCKS)
    def _():
        pltpu.make_async_copy(mid, mid, ur_sem).wait()
        both = jnp.dot(out_tab[...], mid[...].reshape(1024, 128), preferred_element_type=F32)
        forward = (both[: 2 * NB] + both[2 * NB :]).astype(BF16)
        twice = jnp.concatenate([forward, forward], axis=0)
        gsend[...] = jnp.dot(back_tab[...], twice, preferred_element_type=F32).astype(BF16).reshape(ROWS, 16, 128)
        dst = gbuf.at[pl.ds(pl.multiple_of(my_chunk * CR + my_pair * 16, 16), 16),
                      pl.ds(pl.multiple_of(x * STRIP + my_block * 128, 128), 128)]
        pltpu.make_async_copy(gsend.at[row], dst, gr_sem.at[my_chunk]).start()

        @pl.loop(0, NZ)
        def _(k):
            to_z = rem(z + far8(k), NZ)

            def send(dy, dc):
                to_y, to_core = rem(y + dy, NY), core if dc == 0 else 1 - core
                to = device(to_z, x, to_y, to_core)
                pltpu.make_async_remote_copy(
                    src_ref=gsend.at[to[0]], dst_ref=dst, send_sem=gs_sem, recv_sem=gr_sem.at[my_chunk],
                    device_id=to, device_id_type=MESH).start()

            for dy, dc in around:
                send(dy, dc)

            @pl.when(k < NZ - 1)
            def _():
                send(0, 0)

    gathers, swaps = [], []
    for b in range(CHUNKS):
        block = gbuf.at[pl.ds(b * CR, CR), pl.ds(pl.multiple_of(x * STRIP, 128), STRIP)]
        pltpu.make_async_copy(block, block, gr_sem.at[b]).wait()
        for d in (2, 1, 3):
            copy = pltpu.make_async_remote_copy(
                src_ref=block, dst_ref=block, send_sem=as_sem.at[b, d - 1], recv_sem=ar_sem.at[b, d - 1],
                device_id=beside(d), device_id_type=MESH)
            copy.start()
            gathers.append(copy)
    fold = jnp.concatenate([expand, jnp.zeros((256 - TILE, TILE * OWN), BF16)], axis=0)
    own_k = (k_row == k_lane)[:CR]
    lines = jnp.broadcast_to(last[...][:, None, :], (NB // 2, PC, 2 * CR)).reshape(NB // 2 * PC, 2 * CR)
    p_row = lax.broadcasted_iota(jnp.int32, lines.shape, 0) % PC
    p_lane = (lax.broadcasted_iota(jnp.int32, lines.shape, 1) // KC) % PC
    lines = jnp.where(p_row == p_lane, lines, 0.0)
    high = lines.astype(BF16)
    lines = jnp.concatenate([high, (lines - high.astype(F32)).astype(BF16)], axis=1)
    chip = rem(z, 4) * 4 + y

    def swap_of(b):
        for copy in gathers[b * 3 : b * 3 + 3]:
            copy.wait_recv()
        got = lax.dot_general(gbuf[b * CR : (b + 1) * CR, :], flat[...], (((1,), (1,)), ((), ())),
                              preferred_element_type=F32)
        got = jnp.where(own_k, got, 0.0).astype(BF16)
        hx[b, core] = lax.dot_general(got, fold, (((1,), (1,)), ((), ())), preferred_element_type=F32).astype(BF16)
        swap = pltpu.make_async_remote_copy(
            src_ref=hx.at[b, core], dst_ref=hx.at[b, core], send_sem=hs_sem.at[b], recv_sem=hr_sem.at[b],
            device_id=device(z, x, y, 1 - core), device_id_type=MESH)
        swap.start()
        swaps.append(swap)

    def blocks_of(b):
        swaps[b].wait_recv()
        pair = hx[b].reshape(2 * CR, 256)
        got = jnp.dot(lines, jnp.concatenate([pair, pair], axis=0), preferred_element_type=F32)
        got = jnp.concatenate([got[:, :128].reshape(16, PC, 128), got[:, 128:].reshape(16, PC, 128)], axis=1)
        bsend[b] = got.astype(BF16)
        pltpu.make_async_copy(bsend.at[b, chip], brecv.at[b, chip], br_sem.at[b]).start()

        @pl.loop(0, 4)
        def _(k):
            low = rem(rem(z, 4) + 2 + k, 4)
            for dy in FAR4:
                to_y = rem(y + dy, NY)

                def send():
                    pltpu.make_async_remote_copy(
                        src_ref=bsend.at[b, low * 4 + to_y], dst_ref=brecv.at[b, chip],
                        send_sem=bs_sem.at[b], recv_sem=br_sem.at[b],
                        device_id=device(div(z, 4) * 4 + low, x, to_y, core), device_id_type=MESH).start()

                if dy:
                    send()
                else:
                    pl.when(k != 2)(send)

    for b in range(CHUNKS):
        swap_of(b)
        if b:
            blocks_of(b - 1)
    blocks_of(CHUNKS - 1)
    mine = []
    for b in range(CHUNKS):
        pltpu.make_async_copy(brecv.at[b], brecv.at[b], br_sem.at[b]).wait()
        got = jnp.sum(brecv[b].astype(F32), axis=0)
        mine.append(jnp.concatenate([got[:PC], got[PC:]], axis=1))
    mine = jnp.concatenate(mine, axis=0)

    group = lax.broadcasted_iota(jnp.int32, (8, 128), 1) // PS
    gram = lax.dot_general(mine, jnp.concatenate([mine] * 4, axis=0), (((1,), (1,)), ((), ())),
                           precision=HIGHEST, preferred_element_type=F32)
    packed = gram[0:8]
    for n in range(1, 4):
        packed = jnp.where(group == n, gram[n * 8 : n * 8 + 8], packed)

    def add_up(buf, stage):
        some = buf.at[pl.ds(0, 15)]
        pltpu.make_async_copy(some, some, qr_sem.at[stage]).wait()
        return jnp.sum(buf[...], axis=0)

    def share(buf, me, stage, to):
        pltpu.make_async_remote_copy(
            src_ref=buf.at[me], dst_ref=buf.at[me], send_sem=qs_sem.at[stage], recv_sem=qr_sem.at[stage],
            device_id=to, device_id_type=MESH).start()

    gz[z * 2 + core] = packed
    for d in FAR8:
        for dc in (1, 0):
            if d or dc:
                share(gz, z * 2 + core, 0, device(rem(z + d, NZ), x, y, core if dc == 0 else 1 - core))
    packed = add_up(gz, 0)
    gx[x * 4 + y] = packed
    for dx in FAR4:
        for dy in FAR4:
            if dx or dy:
                share(gx, x * 4 + y, 1, device(z, rem(x + dx, NX), rem(y + dy, NY), core))
    packed = add_up(gx, 1)

    turned = [packed] + [pltpu.roll(packed, n * PS, 1) for n in range(1, 4)]
    strips = []
    for n in range(4):
        strip = turned[(4 - n) % 4]
        for g in range(1, 4):
            strip = jnp.where(group == g, turned[(g - n) % 4], strip)
        strips.append(strip)
    gram = jnp.concatenate(strips, axis=0)
    s_row = lax.broadcasted_iota(jnp.int32, (PS, 128), 0)
    s_lane = lax.broadcasted_iota(jnp.int32, (PS, 128), 1)
    eye = jnp.where(s_row == s_lane % PS, 1.0, 0.0)
    scale = jnp.sum(jnp.where(s_row == s_lane, gram, 0.0), keepdims=True) + 1e-06

    def left(a):
        high = a.astype(BF16).astype(F32)
        lane = lax.broadcasted_iota(jnp.int32, a.shape, 1)
        return jnp.where(lane < 64, high, a - high).astype(BF16)

    def right(a):
        high = a.astype(BF16)
        low = (a - high.astype(F32)).astype(BF16)
        return jnp.concatenate([high, low, high, low], axis=0)

    square = gram / scale
    inverse = eye
    for step in range(NSTEPS):
        weight = 1.5 * eye - 0.5 * square
        factor = right(weight)
        both = jnp.dot(left(jnp.concatenate([square, inverse], axis=0)), factor, preferred_element_type=F32)
        inverse = both[PS:]
        if step < NSTEPS - 1:
            square = jnp.dot(left(both[:PS]), factor, preferred_element_type=F32)
    answer = jnp.dot(left(inverse), right(mine), preferred_element_type=F32)
    result[...] = answer[:, :TILE] * (math.sqrt(NB * M) / jnp.sqrt(scale))

    for copy in sends + gathers + swaps:
        copy.wait_send()
    for stage, buf in enumerate((gz, gx)):
        some = buf.at[pl.ds(0, 15)]
        pltpu.make_async_copy(some, some, qs_sem.at[stage]).wait()
    for b in range(CHUNKS):
        rest = bsend.at[b, pl.ds(0, 15)]
        pltpu.make_async_copy(rest, rest, bs_sem.at[b]).wait()

    @pl.when(my_block < BLOCKS)
    def _():
        most = mid.at[pl.ds(0, 47)]
        pltpu.make_async_copy(most, most, us_sem).wait()
        most = mid.at[pl.ds(0, 63)]
        pltpu.make_async_copy(most, most, gs_sem).wait()

    @pl.when(my_block >= BLOCKS)
    def _():
        most = mid.at[pl.ds(0, 48)]
        pltpu.make_async_copy(most, most, us_sem).wait()


def factors(seeds, col):
    lane = np.broadcast_to(np.arange(256, dtype=np.int32), (NB, 256))
    first = (lane < TILE).astype(np.int32)
    base, gap = lane - TILE * (1 - first), 1 + first
    index = base + first * (col * TILE)
    inner = residue(seeds[:, None] * (index + 1)) * (index + 1 + gap)
    return jnp.where(first > 0, residue(inner), inner).astype(F32)


def shards(damping, block_seeds):
    mix, out, back, last = tables()
    vmem, anywhere = pl.BlockSpec(memory_space=pltpu.VMEM), pl.BlockSpec(memory_space=pl.ANY)
    dma = pltpu.SemaphoreType.DMA
    turned = pl.pallas_call(
        kernel,
        out_shape=jax.ShapeDtypeStruct((PS, TILE), F32),
        in_specs=[vmem] + [anywhere] * 5,
        out_specs=vmem,
        scratch_shapes=[
            pltpu.VMEM((TILE, OWN, M), BF16),
            pltpu.VMEM((TILE * OWN, M), BF16),
            pltpu.VMEM((KC, NB * PS), F32),
            pltpu.VMEM((16, 2 * CR), F32),
            pltpu.VMEM((4 * NB, 1024), BF16),
            pltpu.VMEM((512, 4 * NB), BF16),
            pltpu.VMEM((NB * PS, TILE), BF16),
            pltpu.VMEM((CHUNKS, NX, CR, STRIP), BF16),
            pltpu.VMEM((CHUNKS, NX - 1, CR, STRIP), BF16),
            pltpu.VMEM((CHUNKS, CR, STRIP), BF16),
            pltpu.VMEM((64, 16, 128), BF16),
            pltpu.VMEM((ROWS, 16, 128), BF16),
            pltpu.VMEM((PS * KC, M), BF16),
            pltpu.VMEM((CHUNKS, 2, CR, 256), BF16),
            pltpu.VMEM((CHUNKS, 16, 16, 128), BF16),
            pltpu.VMEM((CHUNKS, 16, 16, 128), BF16),
            pltpu.VMEM((16, 8, 128), F32),
            pltpu.VMEM((16, 8, 128), F32),
            pltpu.SemaphoreType.REGULAR, dma((5,)), dma((CHUNKS, 3)), dma((CHUNKS, 3)), dma, dma, dma,
            dma((CHUNKS,)), dma((CHUNKS, 3)), dma((CHUNKS, 3)), dma((CHUNKS,)), dma((CHUNKS,)),
            dma((CHUNKS,)), dma((CHUNKS,)), dma((2,)), dma((2,)),
        ],
        compiler_params=pltpu.CompilerParams(
            collective_id=0, has_side_effects=True, vmem_limit_bytes=(53 << 20) + (13 << 16)),
        name="hankel",
    )(factors(block_seeds, lax.axis_index("col")), damping, jnp.asarray(mix), jnp.asarray(out), jnp.asarray(back), jnp.asarray(last))
    return turned.T[None]


def solution(mesh):
    return jax.shard_map(
        shards,
        mesh=mesh,
        in_specs=(P("col", "row", None), P()),
        out_specs=P("row", "col", None),
        check_vma=False,
    )
```

```python
import functools
import math

import jax
import jax.numpy as jnp
import numpy as np
from jax import lax
from jax.experimental import pallas as pl
from jax.experimental.pallas import tpu as pltpu
from jax.sharding import PartitionSpec as P

NF = 128
M = 1536
PS = 32
NB = 32
NSTEPS = 12
PRIME = 65521
AWAY = 1 << 20
OWN = 4
KC = 2 * OWN
ROWS = 32
TILE = 192
NX, NY, NZ = 4, 4, 8
CHUNKS = 4
PC = PS // CHUNKS
CR = PC * KC
BLOCKS = 3
STRIP = BLOCKS * 128
MESH = pl.DeviceIdType.MESH
F32, BF16 = jnp.float32, jnp.bfloat16
HIGHEST = lax.Precision.HIGHEST


def wave(step, sign):
    freq = np.arange(NF)[:, None] + 0.5
    angle = math.pi * freq * step[None, :] / NF
    window = np.exp(-math.log(3.0) * step / NB)[None, :]
    return np.stack([np.cos(angle) * window, sign * np.sin(angle) * window], 1).reshape(2 * NF, len(step))


def halves(table):
    high = table.astype(jnp.bfloat16)
    low = (table - high.astype(np.float64)).astype(jnp.bfloat16)
    return high, low


def tables():
    step = np.arange(NB).astype(np.float64)
    amp = math.sqrt(2.0 / NF) / math.sqrt(NB * M)
    mix = np.repeat(wave(step, 1.0), PS, axis=1).astype(np.float32)
    same = np.eye(2)
    out = (amp * wave(step, -1.0)).reshape(ROWS, KC, NB)
    out = np.einsum("akj,pq->pjaqk", out, same).reshape(2 * NB, ROWS * 2 * KC)
    out = np.concatenate([out, out], axis=1)
    out = np.concatenate(halves(out), axis=0)
    back = (amp * wave(step + 1.0, 1.0)).reshape(ROWS, KC, NB)
    back = np.einsum("akj,pq->apkqj", back, same).reshape(ROWS * 2 * KC, 2 * NB)
    back = np.concatenate(halves(back), axis=1)
    last = wave(step, -1.0).reshape(ROWS // 2, 2, KC, NB // 2, 2)
    last = last.transpose(0, 4, 3, 1, 2)
    last = np.broadcast_to(last[:, :, :, :, None, :], last.shape[:4] + (PC, KC))
    last = last.reshape(ROWS * (NB // 2), 2 * CR).astype(np.float32)
    return mix, out, back, last


def sine_terms():
    t = np.cos(np.pi * (np.arange(400) + 0.5) / 400) * 0.5
    t = t[t > 0]
    u = t * t
    basis = np.stack([u**n for n in range(5)], 1)
    return [float(v) for v in np.linalg.lstsq(basis, np.sin(np.pi * t) / t, rcond=None)[0]]


SINE = sine_terms()


def residue(x):
    q = (x.astype(F32) * (1.0 / PRIME)).astype(jnp.int32)
    r = x - q * PRIME
    r = jnp.where(r < 0, r + PRIME, r)
    return jnp.where(r >= PRIME, r - PRIME, r)


FAR4 = (2, 1, 3, 0)
FAR8 = (4, 3, 5, 2, 6, 1, 7, 0)


def rem(a, n):
    return lax.rem(a, jnp.int32(n))


def div(a, n):
    return lax.div(a, jnp.int32(n))


def far8(k):
    half = div(k + 1, 2)
    return 4 + half - 2 * half * rem(k, 2)


def place():
    r, c = lax.axis_index("row"), lax.axis_index("col")
    return div(c, 4) * 4 + div(r, 8), rem(c, 4), rem(div(r, 2), 4), rem(r, 2)


def device(z, x, y, core):
    return (rem(z, 4) * 8 + y * 2 + core, div(z, 4) * 4 + x)


def kernel(facts, damp_hbm, mix_hbm, out_hbm, back_hbm, last_hbm, result,
           damp, flat, mix, last, out_tab, back_tab, probes, fsend, xrecv, summed, mid, gsend, gbuf,
           hx, bsend, brecv, gz, gx,
           ready, load_sem, xs_sem, xr_sem, us_sem, ur_sem, gs_sem, gr_sem, as_sem, ar_sem,
           hs_sem, hr_sem, bs_sem, br_sem, qs_sem, qr_sem):
    z, x, y, core = place()
    row = lax.axis_index("row")
    here = z * 8 + y * 2 + core
    my_chunk, my_pair, my_block = core * 2 + rem(z, 2), div(z, 2), rem(y + 4 - div(z, 2), NY)

    def beside(d):
        return device(z, rem(x + d, NX), y, core)

    def plane(dy, dc):
        return device(z, x, rem(y + dy, NY), core if dc == 0 else 1 - core)

    around = [(dy, dc) for dy in FAR4 for dc in (1, 0) if dy or dc]

    loads = [
        pltpu.make_async_copy(damp_hbm, damp, load_sem.at[1]),
        pltpu.make_async_copy(mix_hbm.at[pl.ds(pl.multiple_of(row * KC, KC), KC)], mix, load_sem.at[0]),
        pltpu.make_async_copy(last_hbm.at[pl.ds(pl.multiple_of(row * 16, 16), 16)], last, load_sem.at[2]),
        pltpu.make_async_copy(out_hbm, out_tab, load_sem.at[3]),
        pltpu.make_async_copy(back_hbm, back_tab, load_sem.at[4]),
    ]
    barrier = pltpu.get_barrier_semaphore()
    for d in FAR8[:-1]:
        pl.semaphore_signal(barrier, inc=1, device_id=device(rem(z + d, NZ), x, y, core), device_id_type=MESH)
    for dy, dc in around:
        pl.semaphore_signal(barrier, inc=1, device_id=plane(dy, dc), device_id_type=MESH)
    for d in FAR4[:-1]:
        pl.semaphore_signal(barrier, inc=1, device_id=beside(d), device_id_type=MESH)
    for load in loads:
        load.start()

    pone = (lax.broadcasted_iota(jnp.int32, (PS, 1), 0) + 1).astype(F32)
    second = jnp.transpose(facts[:, 128:])[TILE - 128 : TILE - 128 + PS]
    for j in range(NB):
        phase = facts[j : j + 1, :TILE] * pone + second[:, j : j + 1]
        phase = phase - jnp.floor(phase * (1.0 / PRIME) + 0.5) * PRIME
        t = phase * (1.0 / PRIME)
        u = t * t
        poly = SINE[4]
        for n in (3, 2, 1, 0):
            poly = poly * u + SINE[n]
        sine = poly * t
        probes[j * PS : (j + 1) * PS, :] = (1.0 - 2.0 * sine * sine).astype(BF16)

    loads[1].wait()
    spread = jnp.broadcast_to(mix[...][None], (PS, KC, NB * PS)).reshape(PS * KC, NB * PS)
    r_idx = lax.broadcasted_iota(jnp.int32, (PS * KC, NB * PS), 0) // KC
    l_idx = lax.broadcasted_iota(jnp.int32, (PS * KC, NB * PS), 1) % PS
    spread = jnp.where(r_idx == l_idx, spread, 0.0).astype(BF16)
    terms = jnp.dot(spread, probes[...], preferred_element_type=F32).astype(BF16)
    wide = lax.broadcasted_iota(jnp.int32, (TILE, TILE * OWN), 1) // OWN
    tall = lax.broadcasted_iota(jnp.int32, (TILE, TILE * OWN), 0)
    expand = jnp.where(wide == tall, 1.0, 0.0).astype(BF16)
    k_row = (lax.broadcasted_iota(jnp.int32, (PS * KC, TILE * OWN), 0) % KC) // 2
    k_lane = lax.broadcasted_iota(jnp.int32, (PS * KC, TILE * OWN), 1) % OWN
    terms = jnp.dot(terms, expand, preferred_element_type=F32)
    terms = jnp.where(k_row == k_lane, terms, 0.0).astype(BF16)

    loads[0].wait()
    for n in range(3):
        flat[:, n * 512 : (n + 1) * 512] = damp[:, :, n * 512 : (n + 1) * 512].reshape(TILE * OWN, 512)
    for load in loads[2:]:
        load.wait()
    sends = []
    for b in range(CHUNKS):
        got = jnp.dot(terms[b * CR : (b + 1) * CR], flat[...], preferred_element_type=F32).astype(BF16)
        for q in range(NX):
            fsend[b, q] = got[:, q * STRIP : (q + 1) * STRIP]
        if b == 0:
            pl.semaphore_wait(barrier, 7 + 7 + NX - 1)
        for d in (2, 1, 3):
            copy = pltpu.make_async_remote_copy(
                src_ref=fsend.at[b, rem(x + d, NX)], dst_ref=xrecv.at[b, d - 1],
                send_sem=xs_sem.at[b, d - 1], recv_sem=xr_sem.at[b, d - 1],
                device_id=beside(d), device_id_type=MESH)
            copy.start()
            sends.append(copy)
        if b == 0:
            for dy, dc in around:
                pl.semaphore_signal(ready, inc=1, device_id=plane(dy, dc), device_id_type=MESH)

    pl.semaphore_wait(ready, 7)
    for b in range(CHUNKS):
        total = fsend[b, x].astype(F32)
        for d, at in ((1, 1), (3, 2), (2, 0)):
            sends[b * 3 + at].wait_recv()
            total = total + xrecv[b, d - 1].astype(F32)
        summed[b] = total.astype(BF16)

        @pl.loop(0, 4)
        def _(k):
            pair = rem(div(z, 2) + 2 + k, 4)
            to_z, to_core = pair * 2 + b % 2, b // 2
            for block in range(BLOCKS):
                src = summed.at[b, pl.ds(pl.multiple_of(pair * 16, 16), 16), pl.ds(block * 128, 128)]
                to_y = rem(pair + block, NY)
                mine = jnp.logical_and(jnp.logical_and(to_z == z, to_y == y), to_core == core)

                @pl.when(mine)
                def _():
                    pltpu.make_async_copy(src, mid.at[here], ur_sem).start()

                @pl.when(jnp.logical_not(mine))
                def _():
                    pltpu.make_async_remote_copy(
                        src_ref=src, dst_ref=mid.at[here], send_sem=us_sem, recv_sem=ur_sem,
                        device_id=device(to_z, x, to_y, to_core), device_id_type=MESH).start()

    @pl.when(my_block < BLOCKS)
    def _():
        pltpu.make_async_copy(mid, mid, ur_sem).wait()
        both = jnp.dot(out_tab[...], mid[...].reshape(1024, 128), preferred_element_type=F32)
        forward = (both[: 2 * NB] + both[2 * NB :]).astype(BF16)
        twice = jnp.concatenate([forward, forward], axis=0)
        gsend[...] = jnp.dot(back_tab[...], twice, preferred_element_type=F32).astype(BF16).reshape(ROWS, 16, 128)
        dst = gbuf.at[pl.ds(pl.multiple_of(my_chunk * CR + my_pair * 16, 16), 16),
                      pl.ds(pl.multiple_of(x * STRIP + my_block * 128, 128), 128)]
        pltpu.make_async_copy(gsend.at[row], dst, gr_sem.at[my_chunk]).start()

        @pl.loop(0, NZ)
        def _(k):
            to_z = rem(z + far8(k), NZ)

            def send(dy, dc):
                to_y, to_core = rem(y + dy, NY), core if dc == 0 else 1 - core
                to = device(to_z, x, to_y, to_core)
                pltpu.make_async_remote_copy(
                    src_ref=gsend.at[to[0]], dst_ref=dst, send_sem=gs_sem, recv_sem=gr_sem.at[my_chunk],
                    device_id=to, device_id_type=MESH).start()

            for dy, dc in around:
                send(dy, dc)

            @pl.when(k < NZ - 1)
            def _():
                send(0, 0)

    gathers, swaps = [], []
    for b in range(CHUNKS):
        block = gbuf.at[pl.ds(b * CR, CR), pl.ds(pl.multiple_of(x * STRIP, 128), STRIP)]
        pltpu.make_async_copy(block, block, gr_sem.at[b]).wait()
        for d in (2, 1, 3):
            copy = pltpu.make_async_remote_copy(
                src_ref=block, dst_ref=block, send_sem=as_sem.at[b, d - 1], recv_sem=ar_sem.at[b, d - 1],
                device_id=beside(d), device_id_type=MESH)
            copy.start()
            gathers.append(copy)
    fold = jnp.concatenate([expand, jnp.zeros((256 - TILE, TILE * OWN), BF16)], axis=0)
    own_k = (k_row == k_lane)[:CR]
    lines = jnp.broadcast_to(last[...][:, None, :], (NB // 2, PC, 2 * CR)).reshape(NB // 2 * PC, 2 * CR)
    p_row = lax.broadcasted_iota(jnp.int32, lines.shape, 0) % PC
    p_lane = (lax.broadcasted_iota(jnp.int32, lines.shape, 1) // KC) % PC
    lines = jnp.where(p_row == p_lane, lines, 0.0)
    high = lines.astype(BF16)
    lines = jnp.concatenate([high, (lines - high.astype(F32)).astype(BF16)], axis=1)
    chip = rem(z, 4) * 4 + y

    def swap_of(b):
        for copy in gathers[b * 3 : b * 3 + 3]:
            copy.wait_recv()
        got = lax.dot_general(gbuf[b * CR : (b + 1) * CR, :], flat[...], (((1,), (1,)), ((), ())),
                              preferred_element_type=F32)
        got = jnp.where(own_k, got, 0.0).astype(BF16)
        hx[b, core] = lax.dot_general(got, fold, (((1,), (1,)), ((), ())), preferred_element_type=F32).astype(BF16)
        swap = pltpu.make_async_remote_copy(
            src_ref=hx.at[b, core], dst_ref=hx.at[b, core], send_sem=hs_sem.at[b], recv_sem=hr_sem.at[b],
            device_id=device(z, x, y, 1 - core), device_id_type=MESH)
        swap.start()
        swaps.append(swap)

    def blocks_of(b):
        swaps[b].wait_recv()
        pair = hx[b].reshape(2 * CR, 256)
        got = jnp.dot(lines, jnp.concatenate([pair, pair], axis=0), preferred_element_type=F32)
        got = jnp.concatenate([got[:, :128].reshape(16, PC, 128), got[:, 128:].reshape(16, PC, 128)], axis=1)
        bsend[b] = got.astype(BF16)
        pltpu.make_async_copy(bsend.at[b, chip], brecv.at[b, chip], br_sem.at[b]).start()

        @pl.loop(0, 4)
        def _(k):
            low = rem(rem(z, 4) + 2 + k, 4)
            for dy in FAR4:
                to_y = rem(y + dy, NY)

                def send():
                    pltpu.make_async_remote_copy(
                        src_ref=bsend.at[b, low * 4 + to_y], dst_ref=brecv.at[b, chip],
                        send_sem=bs_sem.at[b], recv_sem=br_sem.at[b],
                        device_id=device(div(z, 4) * 4 + low, x, to_y, core), device_id_type=MESH).start()

                if dy:
                    send()
                else:
                    pl.when(k != 2)(send)

    for b in range(CHUNKS):
        swap_of(b)
        if b:
            blocks_of(b - 1)
    blocks_of(CHUNKS - 1)
    mine = []
    for b in range(CHUNKS):
        pltpu.make_async_copy(brecv.at[b], brecv.at[b], br_sem.at[b]).wait()
        got = jnp.sum(brecv[b].astype(F32), axis=0)
        mine.append(jnp.concatenate([got[:PC], got[PC:]], axis=1))
    mine = jnp.concatenate(mine, axis=0)

    group = lax.broadcasted_iota(jnp.int32, (8, 128), 1) // PS
    gram = lax.dot_general(mine, jnp.concatenate([mine] * 4, axis=0), (((1,), (1,)), ((), ())),
                           precision=HIGHEST, preferred_element_type=F32)
    packed = gram[0:8]
    for n in range(1, 4):
        packed = jnp.where(group == n, gram[n * 8 : n * 8 + 8], packed)

    def add_up(buf, stage):
        some = buf.at[pl.ds(0, 15)]
        pltpu.make_async_copy(some, some, qr_sem.at[stage]).wait()
        return jnp.sum(buf[...], axis=0)

    def share(buf, me, stage, to):
        pltpu.make_async_remote_copy(
            src_ref=buf.at[me], dst_ref=buf.at[me], send_sem=qs_sem.at[stage], recv_sem=qr_sem.at[stage],
            device_id=to, device_id_type=MESH).start()

    gz[z * 2 + core] = packed
    for d in FAR8:
        for dc in (1, 0):
            if d or dc:
                share(gz, z * 2 + core, 0, device(rem(z + d, NZ), x, y, core if dc == 0 else 1 - core))
    packed = add_up(gz, 0)
    gx[x * 4 + y] = packed
    for dx in FAR4:
        for dy in FAR4:
            if dx or dy:
                share(gx, x * 4 + y, 1, device(z, rem(x + dx, NX), rem(y + dy, NY), core))
    packed = add_up(gx, 1)

    turned = [packed] + [pltpu.roll(packed, n * PS, 1) for n in range(1, 4)]
    strips = []
    for n in range(4):
        strip = turned[(4 - n) % 4]
        for g in range(1, 4):
            strip = jnp.where(group == g, turned[(g - n) % 4], strip)
        strips.append(strip)
    gram = jnp.concatenate(strips, axis=0)
    s_row = lax.broadcasted_iota(jnp.int32, (PS, 128), 0)
    s_lane = lax.broadcasted_iota(jnp.int32, (PS, 128), 1)
    eye = jnp.where(s_row == s_lane % PS, 1.0, 0.0)
    scale = jnp.sum(jnp.where(s_row == s_lane, gram, 0.0), keepdims=True) + 1e-06

    def left(a):
        high = a.astype(BF16).astype(F32)
        lane = lax.broadcasted_iota(jnp.int32, a.shape, 1)
        return jnp.where(lane < 64, high, a - high).astype(BF16)

    def right(a):
        high = a.astype(BF16)
        low = (a - high.astype(F32)).astype(BF16)
        return jnp.concatenate([high, low, high, low], axis=0)

    square = gram / scale
    inverse = eye
    for step in range(NSTEPS):
        weight = 1.5 * eye - 0.5 * square
        factor = right(weight)
        both = jnp.dot(left(jnp.concatenate([square, inverse], axis=0)), factor, preferred_element_type=F32)
        inverse = both[PS:]
        if step < NSTEPS - 1:
            square = jnp.dot(left(both[:PS]), factor, preferred_element_type=F32)
    answer = jnp.dot(left(inverse), right(mine), preferred_element_type=F32)
    result[...] = answer[:, :TILE] * (math.sqrt(NB * M) / jnp.sqrt(scale))

    for copy in sends + gathers + swaps:
        copy.wait_send()
    for stage, buf in enumerate((gz, gx)):
        some = buf.at[pl.ds(0, 15)]
        pltpu.make_async_copy(some, some, qs_sem.at[stage]).wait()
    for b in range(CHUNKS):
        rest = bsend.at[b, pl.ds(0, 15)]
        pltpu.make_async_copy(rest, rest, bs_sem.at[b]).wait()

    @pl.when(my_block < BLOCKS)
    def _():
        most = mid.at[pl.ds(0, 47)]
        pltpu.make_async_copy(most, most, us_sem).wait()
        most = mid.at[pl.ds(0, 63)]
        pltpu.make_async_copy(most, most, gs_sem).wait()

    @pl.when(my_block >= BLOCKS)
    def _():
        most = mid.at[pl.ds(0, 48)]
        pltpu.make_async_copy(most, most, us_sem).wait()


def factors(seeds, col):
    lane = np.arange(256, dtype=np.int32)
    code = np.where(lane < TILE, lane, TILE - AWAY - lane).astype(np.int32)
    start = col * TILE
    index = np.broadcast_to(code, (NB, 256)) + start
    first = index >= 0
    index = jnp.where(first, index, start - AWAY - index)
    inner = residue(seeds[:, None] * (index + 1)) * (index + jnp.where(first, 3, 2))
    return jnp.where(first, residue(inner), inner).astype(F32)


def shards(damping, block_seeds):
    mix, out, back, last = tables()
    vmem, anywhere = pl.BlockSpec(memory_space=pltpu.VMEM), pl.BlockSpec(memory_space=pl.ANY)
    dma = pltpu.SemaphoreType.DMA
    turned = pl.pallas_call(
        kernel,
        out_shape=jax.ShapeDtypeStruct((PS, TILE), F32),
        in_specs=[vmem] + [anywhere] * 5,
        out_specs=vmem,
        scratch_shapes=[
            pltpu.VMEM((TILE, OWN, M), BF16),
            pltpu.VMEM((TILE * OWN, M), BF16),
            pltpu.VMEM((KC, NB * PS), F32),
            pltpu.VMEM((16, 2 * CR), F32),
            pltpu.VMEM((4 * NB, 1024), BF16),
            pltpu.VMEM((512, 4 * NB), BF16),
            pltpu.VMEM((NB * PS, TILE), BF16),
            pltpu.VMEM((CHUNKS, NX, CR, STRIP), BF16),
            pltpu.VMEM((CHUNKS, NX - 1, CR, STRIP), BF16),
            pltpu.VMEM((CHUNKS, CR, STRIP), BF16),
            pltpu.VMEM((64, 16, 128), BF16),
            pltpu.VMEM((ROWS, 16, 128), BF16),
            pltpu.VMEM((PS * KC, M), BF16),
            pltpu.VMEM((CHUNKS, 2, CR, 256), BF16),
            pltpu.VMEM((CHUNKS, 16, 16, 128), BF16),
            pltpu.VMEM((CHUNKS, 16, 16, 128), BF16),
            pltpu.VMEM((16, 8, 128), F32),
            pltpu.VMEM((16, 8, 128), F32),
            pltpu.SemaphoreType.REGULAR, dma((5,)), dma((CHUNKS, 3)), dma((CHUNKS, 3)), dma, dma, dma,
            dma((CHUNKS,)), dma((CHUNKS, 3)), dma((CHUNKS, 3)), dma((CHUNKS,)), dma((CHUNKS,)),
            dma((CHUNKS,)), dma((CHUNKS,)), dma((2,)), dma((2,)),
        ],
        compiler_params=pltpu.CompilerParams(
            collective_id=0, has_side_effects=True, vmem_limit_bytes=(53 << 20) + (13 << 16)),
        name="hankel",
    )(factors(block_seeds, lax.axis_index("col")), damping, jnp.asarray(mix), jnp.asarray(out), jnp.asarray(back), jnp.asarray(last))
    return turned.T[None]


def solution(mesh):
    return jax.shard_map(
        shards,
        mesh=mesh,
        in_specs=(P("col", "row", None), P()),
        out_specs=P("row", "col", None),
        check_vma=False,
    )
```

```python
import functools
import math

import jax
import jax.numpy as jnp
import numpy as np
from jax import lax
from jax.experimental import pallas as pl
from jax.experimental.pallas import tpu as pltpu
from jax.sharding import PartitionSpec as P

NF = 128
M = 1536
PS = 32
NB = 32
NSTEPS = 12
PRIME = 65521
OWN = 4
KC = 2 * OWN
ROWS = 32
TILE = 192
NX, NY, NZ = 4, 4, 8
CHUNKS = 4
PC = PS // CHUNKS
CR = PC * KC
BLOCKS = 3
STRIP = BLOCKS * 128
MESH = pl.DeviceIdType.MESH
F32, BF16 = jnp.float32, jnp.bfloat16
HIGHEST = lax.Precision.HIGHEST


def wave(step, sign):
    freq = np.arange(NF)[:, None] + 0.5
    angle = math.pi * freq * step[None, :] / NF
    window = np.exp(-math.log(3.0) * step / NB)[None, :]
    return np.stack([np.cos(angle) * window, sign * np.sin(angle) * window], 1).reshape(2 * NF, len(step))


def halves(table):
    high = table.astype(jnp.bfloat16)
    low = (table - high.astype(np.float64)).astype(jnp.bfloat16)
    return high, low


def tables():
    step = np.arange(NB).astype(np.float64)
    amp = math.sqrt(2.0 / NF) / math.sqrt(NB * M)
    mix = np.repeat(wave(step, 1.0), PS, axis=1).astype(np.float32)
    same = np.eye(2)
    out = (amp * wave(step, -1.0)).reshape(ROWS, KC, NB)
    out = np.einsum("akj,pq->pjaqk", out, same).reshape(2 * NB, ROWS * 2 * KC)
    out = np.concatenate([out, out], axis=1)
    out = np.concatenate(halves(out), axis=0)
    back = (amp * wave(step + 1.0, 1.0)).reshape(ROWS, KC, NB)
    back = np.einsum("akj,pq->apkqj", back, same).reshape(ROWS * 2 * KC, 2 * NB)
    back = np.concatenate(halves(back), axis=1)
    last = wave(step, -1.0).reshape(ROWS // 2, 2, KC, NB // 2, 2)
    last = last.transpose(0, 4, 3, 1, 2)
    last = np.broadcast_to(last[:, :, :, :, None, :], last.shape[:4] + (PC, KC))
    last = last.reshape(ROWS * (NB // 2), 2 * CR).astype(np.float32)
    return mix, out, back, last


def sine_terms():
    t = np.cos(np.pi * (np.arange(400) + 0.5) / 400) * 0.5
    t = t[t > 0]
    u = t * t
    basis = np.stack([u**n for n in range(5)], 1)
    return [float(v) for v in np.linalg.lstsq(basis, np.sin(np.pi * t) / t, rcond=None)[0]]


SINE = sine_terms()


def residue(x):
    q = (x.astype(F32) * (1.0 / PRIME)).astype(jnp.int32)
    r = x - q * PRIME
    r = jnp.where(r < 0, r + PRIME, r)
    return jnp.where(r >= PRIME, r - PRIME, r)


FAR4 = (2, 1, 3, 0)
FAR8 = (4, 3, 5, 2, 6, 1, 7, 0)


def rem(a, n):
    return lax.rem(a, jnp.int32(n))


def div(a, n):
    return lax.div(a, jnp.int32(n))


def far8(k):
    half = div(k + 1, 2)
    return 4 + half - 2 * half * rem(k, 2)


def place():
    r, c = lax.axis_index("row"), lax.axis_index("col")
    return div(c, 4) * 4 + div(r, 8), rem(c, 4), rem(div(r, 2), 4), rem(r, 2)


def device(z, x, y, core):
    return (rem(z, 4) * 8 + y * 2 + core, div(z, 4) * 4 + x)


def kernel(facts, damp_hbm, mix_hbm, out_hbm, back_hbm, last_hbm, result,
           damp, flat, mix, last, out_tab, back_tab, probes, fsend, xrecv, summed, mid, gsend, gbuf,
           hx, bsend, brecv, gz, gx,
           ready, load_sem, xs_sem, xr_sem, us_sem, ur_sem, gs_sem, gr_sem, as_sem, ar_sem,
           hs_sem, hr_sem, bs_sem, br_sem, qs_sem, qr_sem):
    z, x, y, core = place()
    row = lax.axis_index("row")
    here = z * 8 + y * 2 + core
    my_chunk, my_pair, my_block = core * 2 + rem(z, 2), div(z, 2), rem(y + 4 - div(z, 2), NY)

    def beside(d):
        return device(z, rem(x + d, NX), y, core)

    def plane(dy, dc):
        return device(z, x, rem(y + dy, NY), core if dc == 0 else 1 - core)

    around = [(dy, dc) for dy in FAR4 for dc in (1, 0) if dy or dc]

    loads = [
        pltpu.make_async_copy(damp_hbm, damp, load_sem.at[1]),
        pltpu.make_async_copy(mix_hbm.at[pl.ds(pl.multiple_of(row * KC, KC), KC)], mix, load_sem.at[0]),
        pltpu.make_async_copy(last_hbm.at[pl.ds(pl.multiple_of(row * 16, 16), 16)], last, load_sem.at[2]),
        pltpu.make_async_copy(out_hbm, out_tab, load_sem.at[3]),
        pltpu.make_async_copy(back_hbm, back_tab, load_sem.at[4]),
    ]
    barrier = pltpu.get_barrier_semaphore()
    for d in FAR8[:-1]:
        pl.semaphore_signal(barrier, inc=1, device_id=device(rem(z + d, NZ), x, y, core), device_id_type=MESH)
    for dy, dc in around:
        pl.semaphore_signal(barrier, inc=1, device_id=plane(dy, dc), device_id_type=MESH)
    for d in FAR4[:-1]:
        pl.semaphore_signal(barrier, inc=1, device_id=beside(d), device_id_type=MESH)
    for load in loads:
        load.start()

    pone = (lax.broadcasted_iota(jnp.int32, (PS, 1), 0) + 1).astype(F32)
    second = jnp.transpose(facts[:, 128:])[TILE - 128 : TILE - 128 + PS]
    for j in range(NB):
        phase = facts[j : j + 1, :TILE] * pone + second[:, j : j + 1]
        phase = phase - jnp.floor(phase * (1.0 / PRIME) + 0.5) * PRIME
        t = phase * (1.0 / PRIME)
        u = t * t
        poly = SINE[4]
        for n in (3, 2, 1, 0):
            poly = poly * u + SINE[n]
        sine = poly * t
        probes[j * PS : (j + 1) * PS, :] = (1.0 - 2.0 * sine * sine).astype(BF16)

    loads[1].wait()
    spread = jnp.broadcast_to(mix[...][None], (PS, KC, NB * PS)).reshape(PS * KC, NB * PS)
    r_idx = lax.broadcasted_iota(jnp.int32, (PS * KC, NB * PS), 0) // KC
    l_idx = lax.broadcasted_iota(jnp.int32, (PS * KC, NB * PS), 1) % PS
    spread = jnp.where(r_idx == l_idx, spread, 0.0).astype(BF16)
    terms = jnp.dot(spread, probes[...], preferred_element_type=F32).astype(BF16)
    wide = lax.broadcasted_iota(jnp.int32, (TILE, TILE * OWN), 1) // OWN
    tall = lax.broadcasted_iota(jnp.int32, (TILE, TILE * OWN), 0)
    expand = jnp.where(wide == tall, 1.0, 0.0).astype(BF16)
    k_row = (lax.broadcasted_iota(jnp.int32, (PS * KC, TILE * OWN), 0) % KC) // 2
    k_lane = lax.broadcasted_iota(jnp.int32, (PS * KC, TILE * OWN), 1) % OWN
    terms = jnp.dot(terms, expand, preferred_element_type=F32)
    terms = jnp.where(k_row == k_lane, terms, 0.0).astype(BF16)

    loads[0].wait()
    for n in range(3):
        flat[:, n * 512 : (n + 1) * 512] = damp[:, :, n * 512 : (n + 1) * 512].reshape(TILE * OWN, 512)
    for load in loads[2:]:
        load.wait()
    sends = []
    for b in range(CHUNKS):
        got = jnp.dot(terms[b * CR : (b + 1) * CR], flat[...], preferred_element_type=F32).astype(BF16)
        for q in range(NX):
            fsend[b, q] = got[:, q * STRIP : (q + 1) * STRIP]
        if b == 0:
            pl.semaphore_wait(barrier, 7 + 7 + NX - 1)
        for d in (2, 1, 3):
            copy = pltpu.make_async_remote_copy(
                src_ref=fsend.at[b, rem(x + d, NX)], dst_ref=xrecv.at[b, d - 1],
                send_sem=xs_sem.at[b, d - 1], recv_sem=xr_sem.at[b, d - 1],
                device_id=beside(d), device_id_type=MESH)
            copy.start()
            sends.append(copy)
        if b == 0:
            for dy, dc in around:
                pl.semaphore_signal(ready, inc=1, device_id=plane(dy, dc), device_id_type=MESH)

    pl.semaphore_wait(ready, 7)
    for b in range(CHUNKS):
        total = fsend[b, x].astype(F32)
        for d, at in ((1, 1), (3, 2), (2, 0)):
            sends[b * 3 + at].wait_recv()
            total = total + xrecv[b, d - 1].astype(F32)
        summed[b] = total.astype(BF16)

        @pl.loop(0, 4)
        def _(k):
            pair = rem(div(z, 2) + 2 + k, 4)
            to_z, to_core = pair * 2 + b % 2, b // 2
            for block in range(BLOCKS):
                src = summed.at[b, pl.ds(pl.multiple_of(pair * 16, 16), 16), pl.ds(block * 128, 128)]
                to_y = rem(pair + block, NY)
                mine = jnp.logical_and(jnp.logical_and(to_z == z, to_y == y), to_core == core)

                @pl.when(mine)
                def _():
                    pltpu.make_async_copy(src, mid.at[here], ur_sem).start()

                @pl.when(jnp.logical_not(mine))
                def _():
                    pltpu.make_async_remote_copy(
                        src_ref=src, dst_ref=mid.at[here], send_sem=us_sem, recv_sem=ur_sem,
                        device_id=device(to_z, x, to_y, to_core), device_id_type=MESH).start()

    @pl.when(my_block < BLOCKS)
    def _():
        pltpu.make_async_copy(mid, mid, ur_sem).wait()
        both = jnp.dot(out_tab[...], mid[...].reshape(1024, 128), preferred_element_type=F32)
        forward = (both[: 2 * NB] + both[2 * NB :]).astype(BF16)
        twice = jnp.concatenate([forward, forward], axis=0)
        gsend[...] = jnp.dot(back_tab[...], twice, preferred_element_type=F32).astype(BF16).reshape(ROWS, 16, 128)
        dst = gbuf.at[pl.ds(pl.multiple_of(my_chunk * CR + my_pair * 16, 16), 16),
                      pl.ds(pl.multiple_of(x * STRIP + my_block * 128, 128), 128)]
        pltpu.make_async_copy(gsend.at[row], dst, gr_sem.at[my_chunk]).start()

        @pl.loop(0, NZ)
        def _(k):
            to_z = rem(z + far8(k), NZ)

            def send(dy, dc):
                to_y, to_core = rem(y + dy, NY), core if dc == 0 else 1 - core
                to = device(to_z, x, to_y, to_core)
                pltpu.make_async_remote_copy(
                    src_ref=gsend.at[to[0]], dst_ref=dst, send_sem=gs_sem, recv_sem=gr_sem.at[my_chunk],
                    device_id=to, device_id_type=MESH).start()

            for dy, dc in around:
                send(dy, dc)

            @pl.when(k < NZ - 1)
            def _():
                send(0, 0)

    gathers, swaps = [], []
    for b in range(CHUNKS):
        block = gbuf.at[pl.ds(b * CR, CR), pl.ds(pl.multiple_of(x * STRIP, 128), STRIP)]
        pltpu.make_async_copy(block, block, gr_sem.at[b]).wait()
        for d in (2, 1, 3):
            copy = pltpu.make_async_remote_copy(
                src_ref=block, dst_ref=block, send_sem=as_sem.at[b, d - 1], recv_sem=ar_sem.at[b, d - 1],
                device_id=beside(d), device_id_type=MESH)
            copy.start()
            gathers.append(copy)
    fold = jnp.concatenate([expand, jnp.zeros((256 - TILE, TILE * OWN), BF16)], axis=0)
    own_k = (k_row == k_lane)[:CR]
    lines = jnp.broadcast_to(last[...][:, None, :], (NB // 2, PC, 2 * CR)).reshape(NB // 2 * PC, 2 * CR)
    p_row = lax.broadcasted_iota(jnp.int32, lines.shape, 0) % PC
    p_lane = (lax.broadcasted_iota(jnp.int32, lines.shape, 1) // KC) % PC
    lines = jnp.where(p_row == p_lane, lines, 0.0)
    high = lines.astype(BF16)
    lines = jnp.concatenate([high, (lines - high.astype(F32)).astype(BF16)], axis=1)
    chip = rem(z, 4) * 4 + y

    def swap_of(b):
        for copy in gathers[b * 3 : b * 3 + 3]:
            copy.wait_recv()
        got = lax.dot_general(gbuf[b * CR : (b + 1) * CR, :], flat[...], (((1,), (1,)), ((), ())),
                              preferred_element_type=F32)
        got = jnp.where(own_k, got, 0.0).astype(BF16)
        hx[b, core] = lax.dot_general(got, fold, (((1,), (1,)), ((), ())), preferred_element_type=F32).astype(BF16)
        swap = pltpu.make_async_remote_copy(
            src_ref=hx.at[b, core], dst_ref=hx.at[b, core], send_sem=hs_sem.at[b], recv_sem=hr_sem.at[b],
            device_id=device(z, x, y, 1 - core), device_id_type=MESH)
        swap.start()
        swaps.append(swap)

    def blocks_of(b):
        swaps[b].wait_recv()
        pair = hx[b].reshape(2 * CR, 256)
        got = jnp.dot(lines, jnp.concatenate([pair, pair], axis=0), preferred_element_type=F32)
        got = jnp.concatenate([got[:, :128].reshape(16, PC, 128), got[:, 128:].reshape(16, PC, 128)], axis=1)
        bsend[b] = got.astype(BF16)
        pltpu.make_async_copy(bsend.at[b, chip], brecv.at[b, chip], br_sem.at[b]).start()

        @pl.loop(0, 4)
        def _(k):
            low = rem(rem(z, 4) + 2 + k, 4)
            for dy in FAR4:
                to_y = rem(y + dy, NY)

                def send():
                    pltpu.make_async_remote_copy(
                        src_ref=bsend.at[b, low * 4 + to_y], dst_ref=brecv.at[b, chip],
                        send_sem=bs_sem.at[b], recv_sem=br_sem.at[b],
                        device_id=device(div(z, 4) * 4 + low, x, to_y, core), device_id_type=MESH).start()

                if dy:
                    send()
                else:
                    pl.when(k != 2)(send)

    for b in range(CHUNKS):
        swap_of(b)
        if b:
            blocks_of(b - 1)
    blocks_of(CHUNKS - 1)
    mine = []
    for b in range(CHUNKS):
        pltpu.make_async_copy(brecv.at[b], brecv.at[b], br_sem.at[b]).wait()
        got = jnp.sum(brecv[b].astype(F32), axis=0)
        mine.append(jnp.concatenate([got[:PC], got[PC:]], axis=1))
    mine = jnp.concatenate(mine, axis=0)

    group = lax.broadcasted_iota(jnp.int32, (8, 128), 1) // PS
    gram = lax.dot_general(mine, jnp.concatenate([mine] * 4, axis=0), (((1,), (1,)), ((), ())),
                           precision=HIGHEST, preferred_element_type=F32)
    packed = gram[0:8]
    for n in range(1, 4):
        packed = jnp.where(group == n, gram[n * 8 : n * 8 + 8], packed)

    def add_up(buf, stage):
        some = buf.at[pl.ds(0, 15)]
        pltpu.make_async_copy(some, some, qr_sem.at[stage]).wait()
        return jnp.sum(buf[...], axis=0)

    def share(buf, me, stage, to):
        pltpu.make_async_remote_copy(
            src_ref=buf.at[me], dst_ref=buf.at[me], send_sem=qs_sem.at[stage], recv_sem=qr_sem.at[stage],
            device_id=to, device_id_type=MESH).start()

    gz[z * 2 + core] = packed
    for d in FAR8:
        for dc in (1, 0):
            if d or dc:
                share(gz, z * 2 + core, 0, device(rem(z + d, NZ), x, y, core if dc == 0 else 1 - core))
    for copy in sends + gathers + swaps:
        copy.wait_send()

    @pl.when(my_block < BLOCKS)
    def _():
        most = mid.at[pl.ds(0, 47)]
        pltpu.make_async_copy(most, most, us_sem).wait()
        most = mid.at[pl.ds(0, 63)]
        pltpu.make_async_copy(most, most, gs_sem).wait()

    @pl.when(my_block >= BLOCKS)
    def _():
        most = mid.at[pl.ds(0, 48)]
        pltpu.make_async_copy(most, most, us_sem).wait()

    packed = add_up(gz, 0)
    gx[x * 4 + y] = packed
    for dx in FAR4:
        for dy in FAR4:
            if dx or dy:
                share(gx, x * 4 + y, 1, device(z, rem(x + dx, NX), rem(y + dy, NY), core))
    for b in range(CHUNKS):
        rest = bsend.at[b, pl.ds(0, 15)]
        pltpu.make_async_copy(rest, rest, bs_sem.at[b]).wait()
    packed = add_up(gx, 1)
    for stage, buf in enumerate((gz, gx)):
        some = buf.at[pl.ds(0, 15)]
        pltpu.make_async_copy(some, some, qs_sem.at[stage]).wait()

    turned = [packed] + [pltpu.roll(packed, n * PS, 1) for n in range(1, 4)]
    strips = []
    for n in range(4):
        strip = turned[(4 - n) % 4]
        for g in range(1, 4):
            strip = jnp.where(group == g, turned[(g - n) % 4], strip)
        strips.append(strip)
    gram = jnp.concatenate(strips, axis=0)
    s_row = lax.broadcasted_iota(jnp.int32, (PS, 128), 0)
    s_lane = lax.broadcasted_iota(jnp.int32, (PS, 128), 1)
    eye = jnp.where(s_row == s_lane % PS, 1.0, 0.0)
    scale = jnp.sum(jnp.where(s_row == s_lane, gram, 0.0), keepdims=True) + 1e-06

    def left(a):
        high = a.astype(BF16).astype(F32)
        lane = lax.broadcasted_iota(jnp.int32, a.shape, 1)
        return jnp.where(lane < 64, high, a - high).astype(BF16)

    def right(a):
        high = a.astype(BF16)
        low = (a - high.astype(F32)).astype(BF16)
        return jnp.concatenate([high, low, high, low], axis=0)

    square = gram / scale
    inverse = eye
    for step in range(NSTEPS):
        weight = 1.5 * eye - 0.5 * square
        factor = right(weight)
        both = jnp.dot(left(jnp.concatenate([square, inverse], axis=0)), factor, preferred_element_type=F32)
        inverse = both[PS:]
        if step < NSTEPS - 1:
            square = jnp.dot(left(both[:PS]), factor, preferred_element_type=F32)
    answer = jnp.dot(left(inverse), right(mine), preferred_element_type=F32)
    result[...] = answer[:, :TILE] * (math.sqrt(NB * M) / jnp.sqrt(scale))


def factors(seeds, col):
    lane = np.broadcast_to(np.arange(256, dtype=np.int32), (NB, 256))
    first = (lane < TILE).astype(np.int32)
    base, gap = lane - TILE * (1 - first), 1 + first
    index = base + first * (col * TILE)
    inner = residue(seeds[:, None] * (index + 1)) * (index + 1 + gap)
    return jnp.where(first > 0, residue(inner), inner).astype(F32)


def shards(damping, block_seeds):
    mix, out, back, last = tables()
    vmem, anywhere = pl.BlockSpec(memory_space=pltpu.VMEM), pl.BlockSpec(memory_space=pl.ANY)
    dma = pltpu.SemaphoreType.DMA
    turned = pl.pallas_call(
        kernel,
        out_shape=jax.ShapeDtypeStruct((PS, TILE), F32),
        in_specs=[vmem] + [anywhere] * 5,
        out_specs=vmem,
        scratch_shapes=[
            pltpu.VMEM((TILE, OWN, M), BF16),
            pltpu.VMEM((TILE * OWN, M), BF16),
            pltpu.VMEM((KC, NB * PS), F32),
            pltpu.VMEM((16, 2 * CR), F32),
            pltpu.VMEM((4 * NB, 1024), BF16),
            pltpu.VMEM((512, 4 * NB), BF16),
            pltpu.VMEM((NB * PS, TILE), BF16),
            pltpu.VMEM((CHUNKS, NX, CR, STRIP), BF16),
            pltpu.VMEM((CHUNKS, NX - 1, CR, STRIP), BF16),
            pltpu.VMEM((CHUNKS, CR, STRIP), BF16),
            pltpu.VMEM((64, 16, 128), BF16),
            pltpu.VMEM((ROWS, 16, 128), BF16),
            pltpu.VMEM((PS * KC, M), BF16),
            pltpu.VMEM((CHUNKS, 2, CR, 256), BF16),
            pltpu.VMEM((CHUNKS, 16, 16, 128), BF16),
            pltpu.VMEM((CHUNKS, 16, 16, 128), BF16),
            pltpu.VMEM((16, 8, 128), F32),
            pltpu.VMEM((16, 8, 128), F32),
            pltpu.SemaphoreType.REGULAR, dma((5,)), dma((CHUNKS, 3)), dma((CHUNKS, 3)), dma, dma, dma,
            dma((CHUNKS,)), dma((CHUNKS, 3)), dma((CHUNKS, 3)), dma((CHUNKS,)), dma((CHUNKS,)),
            dma((CHUNKS,)), dma((CHUNKS,)), dma((2,)), dma((2,)),
        ],
        compiler_params=pltpu.CompilerParams(
            collective_id=0, has_side_effects=True, vmem_limit_bytes=(53 << 20) + (13 << 16)),
        name="hankel",
    )(factors(block_seeds, lax.axis_index("col")), damping, jnp.asarray(mix), jnp.asarray(out), jnp.asarray(back), jnp.asarray(last))
    return turned.T[None]


def solution(mesh):
    return jax.shard_map(
        shards,
        mesh=mesh,
        in_specs=(P("col", "row", None), P()),
        out_specs=P("row", "col", None),
        check_vma=False,
    )
```
